256 devices in a mesh: seq: 32 (over x, z), grp: 8 (over y, core).
Axes of the slice: x: 4, y: 4, z: 8, core: 2. Of those that a mesh axis runs over, the one named last changes fastest.
Arguments:
- queries: bfloat16 [32768, 4096], P(('grp', 'seq')), parts along dimension 0, may hold values from -8.5 to 8.5
- keys: bfloat16 [32768, 512], P(('grp', 'seq')), parts along dimension 0, may hold values from -6 to 6
- values: bfloat16 [32768, 512], P(('grp', 'seq')), parts along dimension 0, may hold values from -6 to 6
- out_grad: bfloat16 [32768, 4096], P(('grp', 'seq')), parts along dimension 0, may hold values from -6 to 6
- doc_lengths: int32 [64], P('grp'), parts along dimension 0, may hold values from 1 to 1024, 4096 in all
- span_order: int32 [512], P('grp'), parts along dimension 0, may hold values from 0 to 63, each once
Outputs:
- attended: bfloat16 [32768, 4096], P(('grp', 'seq')), parts along dimension 0
- grad_q: bfloat16 [32768, 4096], P(('grp', 'seq')), parts along dimension 0
- grad_k: bfloat16 [32768, 512], P(('grp', 'seq')), parts along dimension 0
- grad_v: bfloat16 [32768, 512], P(('grp', 'seq')), parts along dimension 0
The draws below stay inside these ranges and needn't reach their ends.
There are 8 independent parts, one for each index of `grp`. The reference program is written for one: setup_inputs(seed, part) draws one part's arguments, and reference() takes and returns one part's arrays. A program takes and returns all parts, laid end to end along the dimension named above; each array names one. Nothing has to cross between parts.
Inputs may be any that keep to these rules, and one draw needn't show every extreme that they name: `doc_lengths`: the lengths sum to 4096; the longest is exactly 1024. `span_order`: each span number appears once.
All inputs are finite; a program needn't handle non-finite values.
Results may differ from the reference program's by a relative error of at most 0.015.
Values may be sent and summed in bfloat16 or wider, within the bound.
A program may use at most 64 MiB of HBM per device.

```python
import math
import jax
import jax.numpy as jnp
import numpy as np
from jax import lax

QUERY_HEADS = 32
KEY_VALUE_HEADS = 4
HEAD_SIZE = 128
NDOC = 8
PACKED_TOKENS = 4096
NCHUNK = 64


def draw_queries(key, part):
    key = jax.random.fold_in(key, 1)
    base_offset = jax.random.truncated_normal(key, -6.0, 6.0, (PACKED_TOKENS, QUERY_HEADS, HEAD_SIZE), jnp.float32)
    return base_offset.reshape(PACKED_TOKENS, QUERY_HEADS * HEAD_SIZE).astype(jnp.bfloat16)


def draw_keys(key, part):
    key = jax.random.fold_in(key, 2)
    base_offset = jax.random.truncated_normal(key, -6.0, 6.0, (PACKED_TOKENS, KEY_VALUE_HEADS, HEAD_SIZE), jnp.float32)
    return base_offset.reshape(PACKED_TOKENS, KEY_VALUE_HEADS * HEAD_SIZE).astype(jnp.bfloat16)


def block_scale(rng, extent, cuts, least, largest):
    def one(dim, blocks):
        steps = jax.random.uniform(jax.random.fold_in(jax.random.fold_in(rng, 6), dim), (blocks,), jnp.float32, least / len(cuts), largest / len(cuts))
        return jnp.repeat(jnp.exp(steps), extent[dim] // blocks).reshape((-1,) + (1,) * (len(extent) - dim - 1))

    gain = one(*cuts[0])
    for cut in cuts[1:]:
        gain = gain * one(*cut)
    return gain


def length_profile(amount, total, bound, slope):
    portions = [(1 << 20) // math.isqrt(grade ** slope) + 1 for grade in range(2, amount + 1)]
    surplus, holding = total - bound - (amount - 1), [1] * (amount - 1)
    while surplus > 0:
        movable = [i for i in range(amount - 1) if holding[i] < bound]
        pool, remaining = sum([portions[i] for i in movable]), surplus
        for i in movable:
            addition = min(bound - holding[i], max(1, remaining * portions[i] // pool), surplus)
            holding[i] = holding[i] + addition
            surplus = surplus - addition
    return np.array([bound] + holding)


def ragged_sizes(key, number_of, total, bound, skew):
    if number_of == 2:
        one = jax.random.randint(key, (), max(1, total - bound), min(bound, total - 1) + 1)
        return jnp.stack([one, total - one])
    sizes = jnp.asarray(length_profile(number_of, total, bound, skew), jnp.int32)
    pairs = (number_of - 1) // 2
    giver, taker = sizes[1:1 + 2 * pairs:2], sizes[2:2 + 2 * pairs:2]
    margin = jnp.minimum(giver - 1, bound - taker)
    passed = jax.random.randint(jax.random.fold_in(key, 1), (pairs,), 0, 1 << 20) % (margin + 1)
    sizes = sizes.at[1:1 + 2 * pairs:2].set(giver - passed).at[2:2 + 2 * pairs:2].set(taker + passed)
    return sizes[jax.random.permutation(jax.random.fold_in(key, 2), number_of)]


def bell_draw(stream_key, shape, width, reach, shards=(), held_as=jnp.bfloat16):
    values = width * jax.random.normal(stream_key, shape, jnp.float32)
    if shards:
        values = values * block_scale(stream_key, shape, shards, -0.22, 0.18)
    return jnp.clip(values, -reach, reach).astype(held_as)


def setup_inputs(seed: int = 0, part: int = 0) -> dict:
    key_list = jax.random.split(jax.random.key(seed), 7)
    part_splits = jax.random.split(jax.random.fold_in(key_list[6], part), 7)
    queries = draw_queries(jax.random.fold_in(jax.random.fold_in(key_list[6], part), 71), part)
    keys = draw_keys(jax.random.fold_in(jax.random.fold_in(key_list[6], part), 71), part)
    values = bell_draw(part_splits[2], (PACKED_TOKENS, KEY_VALUE_HEADS * HEAD_SIZE), 1.0, 6.0, ((0, 32),))
    out_grad = bell_draw(part_splits[3], (PACKED_TOKENS, QUERY_HEADS * HEAD_SIZE), 1.0, 6.0, ((0, 32),))
    doc_lengths = ragged_sizes(part_splits[4], NDOC, PACKED_TOKENS, PACKED_TOKENS // 4, 2).astype(jnp.int32)
    span_order = jax.random.permutation(part_splits[5], NCHUNK).astype(jnp.int32)
    return {"queries": queries, "keys": keys, "values": values, "out_grad": out_grad, "doc_lengths": doc_lengths, "span_order": span_order}


def reference(queries, keys, values, out_grad, doc_lengths, span_order):
    packed_length = queries.shape[0]
    spans = span_order.shape[0]
    half = packed_length // spans
    inverse = jnp.argsort(span_order).astype(jnp.int32)

    def into_placement(block_tile):
        return block_tile.reshape(spans, half, block_tile.shape[1])[inverse].reshape(packed_length, block_tile.shape[1])

    def into_layout(block_tile):
        return block_tile.reshape(spans, half, block_tile.shape[1])[span_order].reshape(packed_length, block_tile.shape[1])

    starts = jnp.cumsum(doc_lengths) - doc_lengths
    places = jnp.arange(packed_length, dtype=jnp.int32)
    docs = jnp.sum((places[:, None] >= starts[None, 1:]).astype(jnp.int32), axis=1)
    visible = (places[None, :] <= places[:, None]) & (docs[None, :] == docs[:, None])
    head_group = QUERY_HEADS // KEY_VALUE_HEADS
    scale = HEAD_SIZE ** -0.5
    q_all = into_placement(queries).reshape(packed_length, QUERY_HEADS, HEAD_SIZE).transpose(1, 0, 2)
    key_matrix = into_placement(keys).reshape(packed_length, KEY_VALUE_HEADS, HEAD_SIZE).transpose(1, 0, 2)
    value_matrix = into_placement(values).reshape(packed_length, KEY_VALUE_HEADS, HEAD_SIZE).transpose(1, 0, 2)
    g_all = into_placement(out_grad).reshape(packed_length, QUERY_HEADS, HEAD_SIZE).transpose(1, 0, 2)

    def one_head(head):
        q_head = q_all[head]
        k_head = key_matrix[head // head_group]
        v_head = value_matrix[head // head_group]
        g_head = g_all[head]
        scores = jnp.dot(q_head, k_head.T, preferred_element_type=jnp.float32) * scale
        scores = jnp.where(visible, scores, -1e30)
        top = jnp.max(scores, axis=1, keepdims=True)
        weights = jnp.where(visible, jnp.exp(scores - top), 0.0)
        total = jnp.sum(weights, axis=1, keepdims=True)
        probs = weights / total
        rounded = probs.astype(jnp.bfloat16)
        output = jnp.dot(rounded, v_head, preferred_element_type=jnp.float32).astype(jnp.bfloat16)
        delta = jnp.sum(output.astype(jnp.float32) * g_head.astype(jnp.float32), axis=1, keepdims=True)
        pressure = jnp.dot(g_head, v_head.T, preferred_element_type=jnp.float32)
        slopes = (probs * (pressure - delta)).astype(jnp.bfloat16)
        q_grad = (jnp.dot(slopes, k_head, preferred_element_type=jnp.float32) * scale).astype(jnp.bfloat16)
        k_grad = jnp.dot(slopes.T, q_head, preferred_element_type=jnp.float32) * scale
        v_grad = jnp.dot(rounded.T, g_head, preferred_element_type=jnp.float32)
        return output, q_grad, k_grad, v_grad

    outputs, q_grads, k_grads, v_grads = lax.map(one_head, jnp.arange(QUERY_HEADS, dtype=jnp.int32))
    attended = into_layout(outputs.transpose(1, 0, 2).reshape(packed_length, QUERY_HEADS * HEAD_SIZE))
    grad_q = into_layout(q_grads.transpose(1, 0, 2).reshape(packed_length, QUERY_HEADS * HEAD_SIZE))

    def narrow(stack_parts):
        group_summed = jnp.sum(stack_parts.reshape(KEY_VALUE_HEADS, head_group, packed_length, HEAD_SIZE), axis=1)
        return into_layout(group_summed.transpose(1, 0, 2).reshape(packed_length, KEY_VALUE_HEADS * HEAD_SIZE)).astype(jnp.bfloat16)

    return attended, grad_q, narrow(k_grads), narrow(v_grads)
```

```python
import functools
import math

import jax
import jax.numpy as jnp
from jax import lax
from jax.experimental import pallas as pl
from jax.experimental.pallas import tpu as pltpu
from jax.sharding import PartitionSpec as P

NX = 4
NZ = 8
ROWS = 128
SPAN = 64
HEAD = 128
GROUP = 8
WIDE = GROUP * HEAD
SPANS = 64
REACH = 16
MESH = pl.DeviceIdType.MESH
SCALE = HEAD ** -0.5
NEG = -1e30
BF = jnp.bfloat16
F32 = jnp.float32


def place():
    me = lax.axis_index("seq")
    return me // NZ, lax.rem(me, NZ)


def device(x, z):
    return {"seq": lax.rem(x + NX, NX) * NZ + lax.rem(z + NZ, NZ)}


def enter(x, z):
    barrier = pltpu.get_barrier_semaphore()
    partners = [device(x + d, z) for d in (1, 2, 3)] + [device(x, z + 1), device(x, z - 1)]
    for partner in partners:
        pl.semaphore_signal(barrier, inc=1, device_id=partner, device_id_type=MESH)
    pl.semaphore_wait(barrier, len(partners))


def columns(index, width):
    return pl.ds(pl.multiple_of(index * width, width), width)


def ring(arrays):
    return [(a, d, NZ // 2 if a == d else NZ // 2 - 1) for a in range(arrays) for d in (0, 1)]


def gather_kernel(q_ref, k_ref, v_ref, g_ref, qo_ref, ko_ref, vo_ref, go_ref,
                  own_sem, send_sem, recv_sem, ring_send, ring_recv):
    x, z = place()
    enter(x, z)
    sources = [k_ref, v_ref, q_ref, g_ref]
    widths = [HEAD, HEAD, WIDE, WIDE]
    targets = [ko_ref.at[z, x], vo_ref.at[z, x], qo_ref.at[x], go_ref.at[x]]
    copies, local = [], []
    for a in range(4):
        own = pltpu.make_async_copy(sources[a].at[:, columns(x, widths[a])], targets[a], own_sem.at[a])
        own.start()
        local.append(own)
        row = []
        for d in (1, 3, 2):
            to = lax.rem(x + d, NX)
            copy = pltpu.make_async_remote_copy(
                src_ref=sources[a].at[:, columns(to, widths[a])],
                dst_ref=targets[a],
                send_sem=send_sem.at[a, d - 1],
                recv_sem=recv_sem.at[a, d - 1],
                device_id=device(to, z),
                device_id_type=MESH,
            )
            copy.start()
            row.append(copy)
        copies.append(row)

    outs = [ko_ref, vo_ref]

    def hop(a, d, step):
        sign = 1 - 2 * d
        block = lax.rem(z - sign * step + NZ, NZ)
        return pltpu.make_async_remote_copy(
            src_ref=outs[a].at[block],
            dst_ref=outs[a].at[block],
            send_sem=ring_send.at[a, d, step],
            recv_sem=ring_recv.at[a, d, step],
            device_id=device(x, z + sign),
            device_id_type=MESH,
        )

    hops = {}
    for a in range(2):
        local[a].wait()
        for copy in copies[a]:
            copy.wait_recv()
        for d in range(2):
            hops[a, d, 0] = hop(a, d, 0)
            hops[a, d, 0].start()
    for step in range(1, NZ // 2 + 1):
        for a, d, count in ring(2):
            if step <= count:
                hops[a, d, step - 1].wait_recv()
            if step < count:
                hops[a, d, step] = hop(a, d, step)
                hops[a, d, step].start()
    for a in (2, 3):
        local[a].wait()
        for copy in copies[a]:
            copy.wait_recv()
    for row in copies:
        for copy in row:
            copy.wait_send()
    for copy in hops.values():
        copy.wait_send()


def scatter_kernel(o_ref, dq_ref, dk_ref, dv_ref, oo_ref, dqo_ref, dko_ref, dvo_ref,
                   outgoing, incoming, total, own_sem, send_sem, recv_sem, ring_send, ring_recv):
    x, z = place()
    enter(x, z)
    sources = [total.at[0], total.at[1], o_ref, dq_ref]
    widths = [HEAD, HEAD, WIDE, WIDE]
    targets = [dko_ref, dvo_ref, oo_ref, dqo_ref]
    copies, local = [], []

    def exchange(a):
        mine = targets[a].at[:, columns(x, widths[a])]
        own = pltpu.make_async_copy(sources[a].at[x], mine, own_sem.at[a])
        own.start()
        local.append(own)
        for d in (1, 3, 2):
            to = lax.rem(x + d, NX)
            copy = pltpu.make_async_remote_copy(
                src_ref=sources[a].at[to],
                dst_ref=mine,
                send_sem=send_sem.at[a, d - 1],
                recv_sem=recv_sem.at[a, d - 1],
                device_id=device(to, z),
                device_id_type=MESH,
            )
            copy.start()
            copies.append(copy)

    terms = [dk_ref, dv_ref]

    def hop(a, d, step):
        sign = 1 - 2 * d
        return pltpu.make_async_remote_copy(
            src_ref=outgoing.at[a, d, step],
            dst_ref=incoming.at[a, d, step],
            send_sem=ring_send.at[a, d, step],
            recv_sem=ring_recv.at[a, d, step],
            device_id=device(x, z + sign),
            device_id_type=MESH,
        )

    hops = {}
    for step in range(NZ // 2 + 1):
        for a, d, count in ring(2):
            if step > count:
                continue
            if step > 0:
                hops[a, d, step - 1].wait_recv()
            if step < count:
                sign = 1 - 2 * d
                block = lax.rem(z + sign * (count - step) + NZ, NZ)
                value = terms[a][block]
                if step > 0:
                    value = value + incoming[a, d, step - 1].astype(F32)
                outgoing[a, d, step] = value.astype(BF)
                hops[a, d, step] = hop(a, d, step)
                hops[a, d, step].start()
        if step == 0:
            exchange(2)
            exchange(3)
    for a in range(2):
        value = terms[a][z]
        for b, d, count in ring(2):
            if a == b:
                value = value + incoming[a, d, count - 1].astype(F32)
        total[a] = value.astype(BF)
        exchange(a)
    for copy in local:
        copy.wait()
    for copy in copies:
        copy.wait()
    for copy in hops.values():
        copy.wait_send()


def attend_kernel(order_ref, length_ref, q_ref, g_ref, k_ref, v_ref, o_ref, dq_ref, dk_ref, dv_ref,
                  kpos, vpos, dka, dva):
    _, z = place()
    pad = REACH * SPAN
    kpos[:pad] = jnp.zeros((pad, HEAD), BF)
    vpos[:pad] = jnp.zeros((pad, HEAD), BF)
    dka[...] = jnp.zeros(dka.shape, F32)
    dva[...] = jnp.zeros(dva.shape, F32)

    def slot(u):
        zz, rest = u // (2 * NX), lax.rem(u, 2 * NX)
        return 2 * (rest // 2 * NZ + zz) + lax.rem(rest, 2)

    def rows(position):
        return pl.ds(pl.multiple_of((position + REACH) * SPAN, SPAN), SPAN)

    @pl.loop(0, SPANS)
    def _(u):
        here = rows(order_ref[slot(u)])
        kpos[here] = k_ref[u]
        vpos[here] = v_ref[u]

    starts = []
    total = length_ref[0]
    for i in range(1, 8):
        starts.append(total)
        total = total + length_ref[i]

    @pl.loop(0, 2 * NX)
    def _(s):
        xx, half = s // 2, lax.rem(s, 2)
        c = order_ref[2 * (xx * NZ + z) + half]
        lane = lax.broadcasted_iota(jnp.int32, (1, HEAD), 1)
        rp = c * SPAN + lax.rem(lane, SPAN)
        rs = jnp.zeros((1, HEAD), jnp.int32)
        first = jnp.int32(0)
        for start in starts:
            rs = jnp.where(rp >= start, start, rs)
            first = jnp.where(c * SPAN >= start, start, first)
        need = c - first // SPAN + 1
        mine = pl.ds(pl.multiple_of(half * SPAN, SPAN), SPAN)

        def work(width):
            base = pl.multiple_of((c + REACH + 1) * SPAN - width, SPAN)
            window = pl.ds(base, width)
            kp = base - pad + lax.broadcasted_iota(jnp.int32, (width, HEAD), 0)
            seen = (kp >= rs) & (kp <= rp)
            heads = 4
            wide_seen = jnp.concatenate([seen] * (heads // 2), axis=1)

            @pl.loop(0, GROUP // heads)
            def _(part):
                def stacked(ref):
                    return jnp.concatenate(
                        [ref[xx, mine, pl.ds(pl.multiple_of((part * heads + h) * HEAD, HEAD), HEAD)]
                         for h in range(heads)], axis=0)

                kw, vw = kpos[window], vpos[window]
                q, g = stacked(q_ref), stacked(g_ref)
                s_t = lax.dot_general(kw, q, (((1,), (1,)), ((), ())), preferred_element_type=F32)
                s_t = jnp.where(wide_seen, s_t * (SCALE * math.log2(math.e)), NEG)
                e = jnp.exp2(s_t - jnp.max(s_t, axis=0, keepdims=True))
                p = e * (1.0 / jnp.sum(e, axis=0, keepdims=True))
                pb = p.astype(BF)
                o_t = lax.dot_general(vw, pb, (((0,), (0,)), ((), ())), preferred_element_type=F32)
                dva[window] += jnp.dot(pb, g, preferred_element_type=F32)
                dp = lax.dot_general(vw, g, (((1,), (1,)), ((), ())), preferred_element_type=F32)
                delta = jnp.sum(p * dp, axis=0, keepdims=True)
                ds = (p * (dp - delta)).astype(BF)
                dq_t = lax.dot_general(kw, ds, (((0,), (0,)), ((), ())), preferred_element_type=F32)
                dka[window] += jnp.dot(ds, q, preferred_element_type=F32)
                o = o_t.T.astype(BF)
                dq = (dq_t.T * SCALE).astype(BF)
                for h in range(heads):
                    cols = pl.ds(pl.multiple_of((part * heads + h) * HEAD, HEAD), HEAD)
                    o_ref[xx, mine, cols] = o[h * SPAN:(h + 1) * SPAN]
                    dq_ref[xx, mine, cols] = dq[h * SPAN:(h + 1) * SPAN]

        below = 0
        for width in (256, 512, 768, (REACH + 1) * SPAN):
            pl.when((need * SPAN > below) & (need * SPAN <= width))(functools.partial(work, width))
            below = width

    @pl.loop(0, SPANS)
    def _(u):
        here = rows(order_ref[slot(u)])
        dk_ref[u] = dka[here] * SCALE
        dv_ref[u] = dva[here]


def on_device(queries, keys, values, out_grad, doc_lengths, span_order):
    any_spec = pl.BlockSpec(memory_space=pl.ANY)
    vmem = pl.BlockSpec(memory_space=pltpu.VMEM)
    smem = pl.BlockSpec(memory_space=pltpu.SMEM)
    dma = pltpu.SemaphoreType.DMA
    heads_shape = jax.ShapeDtypeStruct((NX, ROWS, WIDE), BF)
    kv_shape = jax.ShapeDtypeStruct((NZ, NX, ROWS, HEAD), BF)
    sems = [dma((4,)), dma((4, 3)), dma((4, 3)), dma((2, 2, 4)), dma((2, 2, 4))]
    q, k, v, g = pl.pallas_call(
        gather_kernel,
        out_shape=[heads_shape, kv_shape, kv_shape, heads_shape],
        in_specs=[any_spec] * 4,
        out_specs=[any_spec] * 4,
        scratch_shapes=sems,
        compiler_params=pltpu.CompilerParams(collective_id=0, has_side_effects=True),
        name="gather",
    )(queries, keys, values, out_grad)

    spans_shape = (SPANS, SPAN, HEAD)
    sum_shape = jax.ShapeDtypeStruct(spans_shape, F32)
    padded = ((SPANS + REACH) * SPAN, HEAD)
    o, dq, dk, dv = pl.pallas_call(
        attend_kernel,
        out_shape=[heads_shape, heads_shape, sum_shape, sum_shape],
        in_specs=[smem, smem] + [vmem] * 4,
        out_specs=[vmem] * 4,
        scratch_shapes=[pltpu.VMEM(padded, BF)] * 2 + [pltpu.VMEM(padded, F32)] * 2,
        compiler_params=pltpu.CompilerParams(vmem_limit_bytes=56 * 2 ** 20),
        name="attend",
    )(span_order, doc_lengths, q, g, k.reshape(spans_shape), v.reshape(spans_shape))

    terms_shape = (NZ, NX, ROWS, HEAD)
    return pl.pallas_call(
        scatter_kernel,
        out_shape=[
            jax.ShapeDtypeStruct((ROWS, NX * WIDE), BF),
            jax.ShapeDtypeStruct((ROWS, NX * WIDE), BF),
            jax.ShapeDtypeStruct((ROWS, NX * HEAD), BF),
            jax.ShapeDtypeStruct((ROWS, NX * HEAD), BF),
        ],
        in_specs=[any_spec, any_spec, vmem, vmem],
        out_specs=[any_spec] * 4,
        scratch_shapes=[
            pltpu.VMEM((2, 2, 4, NX, ROWS, HEAD), BF),
            pltpu.VMEM((2, 2, 4, NX, ROWS, HEAD), BF),
            pltpu.VMEM((2, NX, ROWS, HEAD), BF),
        ] + sems,
        compiler_params=pltpu.CompilerParams(
            collective_id=1, has_side_effects=True, vmem_limit_bytes=32 * 2 ** 20),
        name="scatter",
    )(o, dq, dk.reshape(terms_shape), dv.reshape(terms_shape))


def solution(mesh):
    rows = P(("grp", "seq"), None)
    return jax.shard_map(
        on_device,
        mesh=mesh,
        in_specs=(rows, rows, rows, rows, P("grp"), P("grp")),
        out_specs=(rows, rows, rows, rows),
        check_vma=False,
    )
```

```python
import math

import jax
import jax.numpy as jnp
from jax import lax
from jax.experimental import pallas as pl
from jax.experimental.pallas import tpu as pltpu
from jax.sharding import PartitionSpec as P

NX = 4
NZ = 8
ROWS = 128
SPAN = 64
HEAD = 128
GROUP = 8
WIDE = GROUP * HEAD
SPANS = 64
REACH = 16
PAD = REACH * SPAN
WINDOW = PAD + SPAN
UNITS = 2 * NX
MESH = pl.DeviceIdType.MESH
SCALE = HEAD ** -0.5
NEG = -1e30
BF = jnp.bfloat16
F32 = jnp.float32


def columns(index, width):
    return pl.ds(pl.multiple_of(index * width, width), width)


def product(a, b, contract):
    return lax.dot_general(a, b, ((contract[0], contract[1]), ((), ())), preferred_element_type=F32)


def hop_count(d, j):
    return NZ // 2 if j == d else NZ // 2 - 1


LANES = [(d, j) for j in range(2) for d in range(2)]


def kernel(order_ref, slot_ref, length_ref, q_ref, k_ref, v_ref, g_ref, oo_ref, dqo_ref, dko_ref, dvo_ref,
           qx, gx, kx, vx, kpos, vpos, probs, dkw, dvw, ost, dqst,
           outgoing, incoming, total,
           own_in, send_in, recv_in, own_out, send_out, recv_out, own_fin, send_fin, recv_fin,
           gather_send, gather_recv, ring_send, ring_recv):
    me = lax.axis_index("seq")
    x, z = me // NZ, lax.rem(me, NZ)

    def device(xx, zz):
        return {"seq": lax.rem(xx + NX, NX) * NZ + lax.rem(zz + NZ, NZ)}

    barrier = pltpu.get_barrier_semaphore()
    partners = [device(x + d, z) for d in (1, 2, 3)] + [device(x, z + 1), device(x, z - 1)]
    for partner in partners:
        pl.semaphore_signal(barrier, inc=1, device_id=partner, device_id_type=MESH)
    pl.semaphore_wait(barrier, len(partners))

    sources = [k_ref, v_ref, q_ref, g_ref]
    here = pl.ds((z * NX + x) * 2, 2)
    landing = [kx.at[here], vx.at[here], qx.at[x], gx.at[x]]
    widths = [HEAD, HEAD, WIDE, WIDE]
    inward = []

    def outgoing_columns(a, to):
        return sources[a].at[:, :, columns(to, widths[a])] if a < 2 else sources[a].at[:, columns(to, widths[a])]

    for a in range(4):
        row = [pltpu.make_async_copy(outgoing_columns(a, x), landing[a], own_in.at[a])]
        for d in (1, 3, 2):
            to = lax.rem(x + d, NX)
            row.append(pltpu.make_async_remote_copy(
                src_ref=outgoing_columns(a, to),
                dst_ref=landing[a],
                send_sem=send_in.at[a, d - 1],
                recv_sem=recv_in.at[a, d - 1],
                device_id=device(to, z),
                device_id_type=MESH,
            ))
        for copy in row:
            copy.start()
        inward.append(row)

    def arrived(a):
        inward[a][0].wait()
        for copy in inward[a][1:]:
            copy.wait_recv()

    gathered = [kx, vx]
    gather_hops = {}

    def gather_step(a, step):
        for d, j in LANES:
            count = hop_count(d, j)
            if 0 < step <= count:
                gather_hops[a, d, j, step - 1].wait_recv()
            if step < count:
                sign = 1 - 2 * d
                begin = lax.rem(z - sign * step + NZ, NZ) * 2 * NX + 4 * j
                block = gathered[a].at[pl.ds(begin, 4)]
                gather_hops[a, d, j, step] = pltpu.make_async_remote_copy(
                    src_ref=block,
                    dst_ref=block,
                    send_sem=gather_send.at[a, d, j, step],
                    recv_sem=gather_recv.at[a, d, j, step],
                    device_id=device(x, z + sign),
                    device_id_type=MESH,
                )
                gather_hops[a, d, j, step].start()

    arrived(0)
    gather_step(0, 0)

    kpos[:REACH] = jnp.zeros((REACH, SPAN, HEAD), BF)
    vpos[:REACH] = jnp.zeros((REACH, SPAN, HEAD), BF)
    for unit in range(UNITS):
        dkw[unit, 0] = jnp.zeros((SPAN, HEAD), F32)
        dkw[unit, REACH + 2] = jnp.zeros((SPAN, HEAD), F32)
        dvw[unit, 0] = jnp.zeros((SPAN, HEAD), F32)
        dvw[unit, REACH + 2] = jnp.zeros((SPAN, HEAD), F32)

    gather_step(0, 1)
    arrived(1)
    gather_step(0, 2)
    gather_step(0, 3)
    gather_step(1, 0)
    gather_step(0, 4)

    def into_positions(source, target):
        @pl.loop(0, SPANS)
        def _(p):
            target[p + REACH] = source[slot_ref[p]]

    def unit_place(i):
        xx = lax.rem(x + 1 + i // 2, NX)
        return xx, lax.rem(i, 2)

    def unit_span(i):
        xx, half = unit_place(i)
        return order_ref[2 * (xx * NZ + z) + half]

    def window(ref, i):
        c = unit_span(i)
        return jnp.concatenate([ref[c + j] for j in range(REACH + 1)], axis=0)

    def stacked(ref, i):
        xx, half = unit_place(i)
        rows = pl.ds(pl.multiple_of(half * SPAN, SPAN), SPAN)
        return jnp.concatenate([ref[xx, rows, h * HEAD:(h + 1) * HEAD] for h in range(GROUP)], axis=0)

    starts = []
    running = length_ref[0]
    for i in range(1, 8):
        starts.append(running)
        running = running + length_ref[i]

    def weigh(i):
        c = unit_span(i)
        row = c * SPAN + lax.rem(lax.broadcasted_iota(jnp.int32, (1, HEAD), 1), SPAN)
        first = jnp.zeros((1, HEAD), jnp.int32)
        for start in starts:
            first = jnp.where(row >= start, start, first)
        key = (c - REACH) * SPAN + lax.broadcasted_iota(jnp.int32, (WINDOW, HEAD), 0)
        seen = (key >= first) & (key <= row)
        scores = product(window(kpos, i), stacked(qx, i), ((1,), (1,)))
        scores = jnp.where(jnp.concatenate([seen] * (GROUP // 2), axis=1), scores * (SCALE * math.log2(math.e)), NEG)
        weights = jnp.exp2(scores - jnp.max(scores, axis=0, keepdims=True))
        probs[i] = (weights * (1.0 / jnp.sum(weights, axis=0, keepdims=True))).astype(BF)

    def value_terms(i):
        dvw[i, 1:REACH + 2] = jnp.dot(
            probs[i], stacked(gx, i), preferred_element_type=F32).reshape(REACH + 1, SPAN, HEAD)

    def put_heads(target, i, value_t):
        value = value_t.T.astype(BF)
        for h in range(GROUP):
            target[i, :, h * HEAD:(h + 1) * HEAD] = value[h * SPAN:(h + 1) * SPAN]

    staged = [ost, dqst]
    results = [oo_ref, dqo_ref]

    def outward(a, i):
        xx, half = unit_place(i)
        rows = pl.ds(pl.multiple_of(half * SPAN, SPAN), SPAN)
        return pltpu.make_async_remote_copy(
            src_ref=staged[a].at[i],
            dst_ref=results[a].at[rows, columns(x, WIDE)],
            send_sem=send_out.at[a, i],
            recv_sem=recv_out.at[a, i],
            device_id=device(xx, z),
            device_id_type=MESH,
        )

    def keep(a, half):
        rows = pl.ds(half * SPAN, SPAN)
        return pltpu.make_async_copy(
            staged[a].at[UNITS - 2 + half], results[a].at[rows, columns(x, WIDE)], own_out.at[a, half])

    def leave(a, i):
        @pl.when(i < UNITS - 2)
        def _():
            outward(a, i).start()

    def attend(i):
        put_heads(ost, i, product(window(vpos, i), probs[i], ((0,), (0,))))
        leave(0, i)

    def slope(i):
        pressure = product(window(vpos, i), stacked(gx, i), ((1,), (1,)))
        p = probs[i].astype(F32)
        delta = jnp.sum(p * pressure, axis=0, keepdims=True)
        slopes = (p * (pressure - delta)).astype(BF)
        probs[i] = slopes
        dkw[i, 1:REACH + 2] = jnp.dot(
            slopes, stacked(qx, i), preferred_element_type=F32).reshape(REACH + 1, SPAN, HEAD)

    def query_grad(i):
        put_heads(dqst, i, product(window(kpos, i), probs[i], ((0,), (0,))) * SCALE)
        leave(1, i)

    terms = [dkw, dvw]
    factors = [SCALE, 1.0]
    ring_hops = {}

    def add_up(a, block, j, arriving, target):
        spans = [unit_span(i) for i in range(UNITS)]

        @pl.loop(0, 4)
        def _(u):
            xi, half = u // 2, lax.rem(u, 2)
            position = order_ref[2 * ((2 * j + xi) * NZ + block) + half]
            value = jnp.zeros((SPAN, HEAD), F32)
            for i in range(UNITS):
                away = jnp.clip(position - spans[i] + REACH + 1, 0, REACH + 2)
                value += terms[a][i, away]
            value *= factors[a]
            rows = pl.ds(pl.multiple_of(half * SPAN, SPAN), SPAN)
            for ref in arriving:
                value += ref[xi, rows].astype(F32)
            target[xi, rows] = value.astype(BF)

    def ring_step(a, step):
        for d, j in LANES:
            count = hop_count(d, j)
            if 0 < step <= count:
                ring_hops[a, d, j, step - 1].wait_recv()
            if step < count:
                sign = 1 - 2 * d
                arriving = [incoming.at[a, d, j, step - 1]] if step > 0 else []
                add_up(a, lax.rem(z + sign * (count - step) + NZ, NZ), j, arriving, outgoing.at[a, d, j, step])
                ring_hops[a, d, j, step] = pltpu.make_async_remote_copy(
                    src_ref=outgoing.at[a, d, j, step],
                    dst_ref=incoming.at[a, d, j, step],
                    send_sem=ring_send.at[a, d, j, step],
                    recv_sem=ring_recv.at[a, d, j, step],
                    device_id=device(x, z + sign),
                    device_id_type=MESH,
                )
                ring_hops[a, d, j, step].start()

    narrow = [dko_ref, dvo_ref]
    finals = []

    def ring_end(a):
        ring_step(a, NZ // 2)
        for j in range(2):
            arriving = [incoming.at[a, d, j, hop_count(d, j) - 1] for d in range(2)]
            add_up(a, z, j, arriving, total.at[a, pl.ds(2 * j, 2)])
        mine = narrow[a].at[:, columns(x, HEAD)]
        finals.append(pltpu.make_async_copy(total.at[a, x], mine, own_fin.at[a]))
        for d in (1, 3, 2):
            to = lax.rem(x + d, NX)
            finals.append(pltpu.make_async_remote_copy(
                src_ref=total.at[a, to],
                dst_ref=mine,
                send_sem=send_fin.at[a, d - 1],
                recv_sem=recv_fin.at[a, d - 1],
                device_id=device(to, z),
                device_id_type=MESH,
            ))
        for copy in finals[-4:]:
            copy.start()

    def each(body, begin=0, end=UNITS):
        pl.loop(begin, end)(body)

    into_positions(kx, kpos)
    arrived(2)
    each(weigh, 0, 4)
    gather_step(1, 1)
    each(weigh, 4, 8)
    gather_step(1, 2)
    gather_step(1, 3)
    arrived(3)
    each(value_terms)
    ring_step(1, 0)
    gather_step(1, 4)
    into_positions(vx, vpos)
    each(attend)
    for half in range(2):
        keep(0, half).start()
    ring_step(1, 1)
    each(slope, 0, 4)
    ring_step(1, 2)
    each(slope, 4, 8)
    ring_step(0, 0)
    ring_step(1, 3)
    each(query_grad, 0, 4)
    ring_step(0, 1)
    ring_end(1)
    each(query_grad, 4, 8)
    for half in range(2):
        keep(1, half).start()
    ring_step(0, 2)
    ring_step(0, 3)
    ring_end(0)

    for row in inward:
        for copy in row[1:]:
            copy.wait_send()
    for copy in list(gather_hops.values()) + list(ring_hops.values()):
        copy.wait_send()
    for a in range(2):
        for half in range(2):
            keep(a, half).wait()

        @pl.loop(0, UNITS - 2)
        def _(i):
            outward(a, i).wait()

    for copy in finals:
        copy.wait()


def on_device(queries, keys, values, out_grad, doc_lengths, span_order):
    any_spec = pl.BlockSpec(memory_space=pl.ANY)
    smem = pl.BlockSpec(memory_space=pltpu.SMEM)
    dma = pltpu.SemaphoreType.DMA
    vmem = pltpu.VMEM
    heads = (NX, ROWS, WIDE)
    gathered = (SPANS, SPAN, HEAD)
    padded = (SPANS + REACH, SPAN, HEAD)
    windows = (UNITS, REACH + 3, SPAN, HEAD)
    stage = (UNITS, SPAN, WIDE)
    ring = (2, 2, 2, NZ // 2)
    places = jnp.arange(SPANS, dtype=jnp.int32)
    blocks = ((places // 2 % NZ) * NX + places // 2 // NZ) * 2 + places % 2
    slots = jnp.sum(jnp.where(span_order[None, :] == places[:, None], blocks[None, :], 0), axis=1)
    return pl.pallas_call(
        kernel,
        out_shape=[jax.ShapeDtypeStruct((ROWS, NX * width), BF) for width in (WIDE, WIDE, HEAD, HEAD)],
        in_specs=[smem] * 3 + [any_spec] * 4,
        out_specs=[any_spec] * 4,
        scratch_shapes=[
            vmem(heads, BF), vmem(heads, BF), vmem(gathered, BF), vmem(gathered, BF),
            vmem(padded, BF), vmem(padded, BF), vmem((UNITS, WINDOW, GROUP * SPAN), BF),
            vmem(windows, F32), vmem(windows, F32), vmem(stage, BF), vmem(stage, BF),
            vmem(ring + (2, ROWS, HEAD), BF), vmem(ring + (2, ROWS, HEAD), BF), vmem((2, NX, ROWS, HEAD), BF),
            dma((4,)), dma((4, 3)), dma((4, 3)),
            dma((2, 2)), dma((2, UNITS - 2)), dma((2, UNITS - 2)),
            dma((2,)), dma((2, 3)), dma((2, 3)),
            dma(ring), dma(ring), dma(ring), dma(ring),
        ],
        compiler_params=pltpu.CompilerParams(
            collective_id=0, has_side_effects=True, vmem_limit_bytes=56 * 2 ** 20),
        name="attention",
    )(span_order, slots, doc_lengths, queries, keys.reshape(2, SPAN, NX * HEAD), values.reshape(2, SPAN, NX * HEAD), out_grad)


def solution(mesh):
    rows = P(("grp", "seq"), None)
    return jax.shard_map(
        lambda *args: tuple(on_device(*args)),
        mesh=mesh,
        in_specs=(rows, rows, rows, rows, P("grp"), P("grp")),
        out_specs=(rows, rows, rows, rows),
        check_vma=False,
    )
```

```python
import math

import jax
import jax.numpy as jnp
from jax import lax
from jax.experimental import pallas as pl
from jax.experimental.pallas import tpu as pltpu
from jax.sharding import PartitionSpec as P

NX = 4
NZ = 8
ROWS = 128
SPAN = 64
HEAD = 128
GROUP = 8
WIDE = GROUP * HEAD
SPANS = 64
REACH = 16
PAD = REACH * SPAN
WINDOW = PAD + SPAN
UNITS = 2 * NX
MESH = pl.DeviceIdType.MESH
SCALE = HEAD ** -0.5
NEG = -1e30
BF = jnp.bfloat16
F32 = jnp.float32


def columns(index, width):
    return pl.ds(pl.multiple_of(index * width, width), width)


def product(a, b, contract):
    return lax.dot_general(a, b, ((contract[0], contract[1]), ((), ())), preferred_element_type=F32)


def hop_count(d, j):
    return NZ // 2 if j == d else NZ // 2 - 1


LANES = [(d, j) for j in range(2) for d in range(2)]


def kernel(order_ref, slot_ref, length_ref, q_ref, k_ref, v_ref, g_ref, oo_ref, dqo_ref, dko_ref, dvo_ref,
           qx, gx, kx, vx, kpos, vpos, probs, dkw, dvw, ost, dqst,
           outgoing, incoming, mine, total,
           own_in, send_in, recv_in, own_out, send_out, recv_out, own_fin, send_fin, recv_fin,
           gather_send, gather_recv, ring_send, ring_recv):
    me = lax.axis_index("seq")
    x, z = me // NZ, lax.rem(me, NZ)

    def device(xx, zz):
        return {"seq": lax.rem(xx + NX, NX) * NZ + lax.rem(zz + NZ, NZ)}

    barrier = pltpu.get_barrier_semaphore()
    partners = [device(x + d, z) for d in (1, 2, 3)] + [device(x, z + 1), device(x, z - 1)]
    for partner in partners:
        pl.semaphore_signal(barrier, inc=1, device_id=partner, device_id_type=MESH)
    pl.semaphore_wait(barrier, len(partners))

    sources = [k_ref, v_ref, q_ref, g_ref]
    here = pl.ds((z * NX + x) * 2, 2)
    landing = [kx.at[here], vx.at[here], qx.at[x], gx.at[x]]
    widths = [HEAD, HEAD, WIDE, WIDE]
    inward = []

    def outgoing_columns(a, to):
        return sources[a].at[:, :, columns(to, widths[a])] if a < 2 else sources[a].at[:, columns(to, widths[a])]

    for a in range(4):
        row = [pltpu.make_async_copy(outgoing_columns(a, x), landing[a], own_in.at[a])]
        for d in (1, 3, 2):
            to = lax.rem(x + d, NX)
            row.append(pltpu.make_async_remote_copy(
                src_ref=outgoing_columns(a, to),
                dst_ref=landing[a],
                send_sem=send_in.at[a, d - 1],
                recv_sem=recv_in.at[a, d - 1],
                device_id=device(to, z),
                device_id_type=MESH,
            ))
        inward.append(row)
    for a in (0, 1):
        for copy in inward[a]:
            copy.start()
    for d in range(4):
        for a in (2, 3):
            inward[a][d].start()

    def arrived(a, which=range(4)):
        for d in which:
            if d == 0:
                inward[a][0].wait()
            else:
                inward[a][d].wait_recv()

    gathered = [kx, vx]

    def gather_hop(a, d, j, step):
        sign = 1 - 2 * d
        block = gathered[a].at[pl.ds(lax.rem(z - sign * step + NZ, NZ) * 2 * NX + 4 * j, 4)]
        return pltpu.make_async_remote_copy(
            src_ref=block,
            dst_ref=block,
            send_sem=gather_send.at[a, d, j, step],
            recv_sem=gather_recv.at[a, d, j, step],
            device_id=device(x, z + sign),
            device_id_type=MESH,
        )

    def gather_step(a, step):
        for d, j in LANES:
            count = hop_count(d, j)
            if 0 < step <= count:
                gather_hop(a, d, j, step - 1).wait_recv()
            if step < count:
                gather_hop(a, d, j, step).start()

    arrived(0)
    gather_step(0, 0)
    arrived(1)
    kpos[:REACH] = jnp.zeros((REACH, SPAN, HEAD), BF)
    vpos[:REACH] = jnp.zeros((REACH, SPAN, HEAD), BF)
    for unit in range(UNITS):
        dkw[unit, 0] = jnp.zeros((SPAN, HEAD), F32)
        dkw[unit, REACH + 2] = jnp.zeros((SPAN, HEAD), F32)
        dvw[unit, 0] = jnp.zeros((SPAN, HEAD), F32)
        dvw[unit, REACH + 2] = jnp.zeros((SPAN, HEAD), F32)

    gather_step(0, 1)
    gather_step(1, 0)
    gather_step(0, 2)
    gather_step(1, 1)
    gather_step(0, 3)
    gather_step(1, 2)
    gather_step(0, 4)

    def into_positions(source, target):
        @pl.loop(0, SPANS)
        def _(p):
            target[p + REACH] = source[slot_ref[p]]

    def unit_place(i):
        t = i // 2
        return lax.rem(x + t + t // 2 - 2 * (t // 3), NX), lax.rem(i, 2)

    def unit_span(i):
        xx, half = unit_place(i)
        return order_ref[2 * (xx * NZ + z) + half]

    def window(ref, i):
        c = unit_span(i)
        return jnp.concatenate([ref[c + j] for j in range(REACH + 1)], axis=0)

    def stacked(ref, i):
        xx, half = unit_place(i)
        rows = pl.ds(pl.multiple_of(half * SPAN, SPAN), SPAN)
        return jnp.concatenate([ref[xx, rows, h * HEAD:(h + 1) * HEAD] for h in range(GROUP)], axis=0)

    starts = []
    running = length_ref[0]
    for i in range(1, 8):
        starts.append(running)
        running = running + length_ref[i]

    def weigh(i):
        c = unit_span(i)
        row = c * SPAN + lax.rem(lax.broadcasted_iota(jnp.int32, (1, HEAD), 1), SPAN)
        first = jnp.zeros((1, HEAD), jnp.int32)
        for start in starts:
            first = jnp.where(row >= start, start, first)
        key = (c - REACH) * SPAN + lax.broadcasted_iota(jnp.int32, (WINDOW, HEAD), 0)
        seen = (key >= first) & (key <= row)
        scores = product(window(kpos, i), stacked(qx, i), ((1,), (1,)))
        scores = jnp.where(jnp.concatenate([seen] * (GROUP // 2), axis=1), scores * (SCALE * math.log2(math.e)), NEG)
        weights = jnp.exp2(scores - jnp.max(scores, axis=0, keepdims=True))
        p = (weights * (1.0 / jnp.sum(weights, axis=0, keepdims=True))).astype(BF)
        probs[i] = p
        dvw[i, 1:REACH + 2] = jnp.dot(
            p, stacked(gx, i), preferred_element_type=F32).reshape(REACH + 1, SPAN, HEAD)

    def put_heads(target, i, value_t):
        value = value_t.T
        for h in range(GROUP):
            target[i, :, h * HEAD:(h + 1) * HEAD] = value[h * SPAN:(h + 1) * SPAN]

    staged = [ost, dqst]
    results = [oo_ref, dqo_ref]

    def outward(a, i):
        xx, half = unit_place(i)
        rows = pl.ds(pl.multiple_of(half * SPAN, SPAN), SPAN)
        return pltpu.make_async_remote_copy(
            src_ref=staged[a].at[i],
            dst_ref=results[a].at[rows, columns(x, WIDE)],
            send_sem=send_out.at[a, i - 2],
            recv_sem=recv_out.at[a, i - 2],
            device_id=device(xx, z),
            device_id_type=MESH,
        )

    def keep(a, half):
        rows = pl.ds(half * SPAN, SPAN)
        return pltpu.make_async_copy(
            staged[a].at[half], results[a].at[rows, columns(x, WIDE)], own_out.at[a, half])

    def attend(i):
        q, g, p = stacked(qx, i), stacked(gx, i), probs[i]
        k, v = window(kpos, i), window(vpos, i)
        o_t = product(v, p, ((0,), (0,))).astype(BF)
        delta = jnp.sum(o_t.astype(F32) * g.T.astype(F32), axis=0, keepdims=True)
        slopes = (p.astype(F32) * (product(v, g, ((1,), (1,))) - delta)).astype(BF)
        dkw[i, 1:REACH + 2] = jnp.dot(
            slopes, q, preferred_element_type=F32).reshape(REACH + 1, SPAN, HEAD)
        put_heads(ost, i, o_t)
        put_heads(dqst, i, (product(k, slopes, ((0,), (0,))) * SCALE).astype(BF))

    terms = [dkw, dvw]
    factors = [SCALE, 1.0]

    def ring_hop(a, d, j, step):
        return pltpu.make_async_remote_copy(
            src_ref=outgoing.at[a, d, j, step],
            dst_ref=incoming.at[a, d, j, step],
            send_sem=ring_send.at[a, d, j, step],
            recv_sem=ring_recv.at[a, d, j, step],
            device_id=device(x, z + 1 - 2 * d),
            device_id_type=MESH,
        )

    def own_terms(a, block, j, target):
        spans = [unit_span(i) for i in range(UNITS)]

        @pl.loop(0, 4)
        def _(u):
            position = order_ref[2 * ((2 * j + u // 2) * NZ + block) + lax.rem(u, 2)]
            value = jnp.zeros((SPAN, HEAD), F32)
            for i in range(UNITS):
                away = jnp.clip(position - spans[i] + REACH + 1, 0, REACH + 2)
                value += terms[a][i, away]
            target[u] = value * factors[a]

    def ring_step(a, step):
        lanes = [(d, j) for d, j in LANES if step < hop_count(d, j)]

        def prepare(d, j):
            sign = 1 - 2 * d
            own_terms(a, lax.rem(z + sign * (hop_count(d, j) - step) + NZ, NZ), j, mine.at[d, j])

        if step > 0:
            for d, j in lanes:
                prepare(d, j)
        for d, j in lanes:
            if step == 0:
                prepare(d, j)
            value = mine[d, j]
            if step > 0:
                ring_hop(a, d, j, step - 1).wait_recv()
                value += incoming[a, d, j, step - 1].astype(F32)
            outgoing[a, d, j, step] = value.astype(BF)
            ring_hop(a, d, j, step).start()

    narrow = [dko_ref, dvo_ref]
    finals = []

    def ring_end(a):
        for j in range(2):
            own_terms(a, z, j, mine.at[0, j])
        for j in range(2):
            value = mine[0, j]
            for d in range(2):
                last = hop_count(d, j) - 1
                ring_hop(a, d, j, last).wait_recv()
                value += incoming[a, d, j, last].astype(F32)
            total[a, 4 * j:4 * j + 4] = value.astype(BF)
        place = narrow[a].at[:, :, columns(x, HEAD)]
        finals.append(pltpu.make_async_copy(total.at[a, pl.ds(2 * x, 2)], place, own_fin.at[a]))
        for d in (1, 3, 2):
            to = lax.rem(x + d, NX)
            finals.append(pltpu.make_async_remote_copy(
                src_ref=total.at[a, pl.ds(2 * to, 2)],
                dst_ref=place,
                send_sem=send_fin.at[a, d - 1],
                recv_sem=recv_fin.at[a, d - 1],
                device_id=device(to, z),
                device_id_type=MESH,
            ))
        for copy in finals[-4:]:
            copy.start()

    into_positions(kx, kpos)

    @pl.loop(0, NX)
    def _(t):
        for k, source in enumerate((0, 2, 1, 3)):
            @pl.when(t == k)
            def _(k=k, source=source):
                arrived(2, (source,))
                arrived(3, (source,))
                if k == 2:
                    gather_step(1, 3)

        weigh(2 * t)
        weigh(2 * t + 1)

    ring_step(1, 0)
    gather_step(1, 4)
    into_positions(vx, vpos)

    @pl.loop(0, NX)
    def _(k):
        t = NX - 1 - k
        for step in (1, 2):
            pl.when(k == step)(lambda step=step: ring_step(1, step))
        attend(2 * t)
        attend(2 * t + 1)

        @pl.when(t > 0)
        def _():
            for half in range(2):
                for a in range(2):
                    outward(a, 2 * t + half).start()

    for a in range(2):
        for half in range(2):
            keep(a, half).start()
    ring_step(0, 0)
    ring_step(1, 3)
    ring_step(0, 1)
    ring_end(1)
    ring_step(0, 2)
    ring_step(0, 3)
    ring_end(0)

    for row in inward:
        for copy in row[1:]:
            copy.wait_send()
    for a in range(2):
        for d, j in LANES:
            for step in range(hop_count(d, j)):
                gather_hop(a, d, j, step).wait_send()
                ring_hop(a, d, j, step).wait_send()
    for a in range(2):
        for half in range(2):
            keep(a, half).wait()

        @pl.loop(2, UNITS)
        def _(i):
            outward(a, i).wait()

    for copy in finals:
        copy.wait()


def on_device(queries, keys, values, out_grad, doc_lengths, span_order):
    any_spec = pl.BlockSpec(memory_space=pl.ANY)
    smem = pl.BlockSpec(memory_space=pltpu.SMEM)
    dma = pltpu.SemaphoreType.DMA
    vmem = pltpu.VMEM
    heads = (NX, ROWS, WIDE)
    gathered = (SPANS, SPAN, HEAD)
    padded = (SPANS + REACH, SPAN, HEAD)
    windows = (UNITS, REACH + 3, SPAN, HEAD)
    stage = (UNITS, SPAN, WIDE)
    ring = (2, 2, 2, NZ // 2)
    piece = (4, SPAN, HEAD)
    places = jnp.arange(SPANS, dtype=jnp.int32)
    blocks = ((places // 2 % NZ) * NX + places // 2 // NZ) * 2 + places % 2
    slots = jnp.sum(jnp.where(span_order[None, :] == places[:, None], blocks[None, :], 0), axis=1)
    attended, grad_q, grad_k, grad_v = pl.pallas_call(
        kernel,
        out_shape=[jax.ShapeDtypeStruct((ROWS, NX * WIDE), BF)] * 2 + [
            jax.ShapeDtypeStruct((2, SPAN, NX * HEAD), BF)] * 2,
        in_specs=[smem] * 3 + [any_spec] * 4,
        out_specs=[any_spec] * 4,
        scratch_shapes=[
            vmem(heads, BF), vmem(heads, BF), vmem(gathered, BF), vmem(gathered, BF),
            vmem(padded, BF), vmem(padded, BF), vmem((UNITS, WINDOW, GROUP * SPAN), BF),
            vmem(windows, F32), vmem(windows, F32), vmem(stage, BF), vmem(stage, BF),
            vmem(ring + piece, BF), vmem(ring + piece, BF), vmem((2, 2) + piece, F32), vmem((2, UNITS, SPAN, HEAD), BF),
            dma((4,)), dma((4, 3)), dma((4, 3)),
            dma((2, 2)), dma((2, UNITS - 2)), dma((2, UNITS - 2)),
            dma((2,)), dma((2, 3)), dma((2, 3)),
            dma(ring), dma(ring), dma(ring), dma(ring),
        ],
        compiler_params=pltpu.CompilerParams(
            collective_id=0, has_side_effects=True, vmem_limit_bytes=56 * 2 ** 20),
        name="attention",
    )(span_order, slots, doc_lengths, queries, keys.reshape(2, SPAN, NX * HEAD), values.reshape(2, SPAN, NX * HEAD), out_grad)
    return attended, grad_q, grad_k.reshape(ROWS, NX * HEAD), grad_v.reshape(ROWS, NX * HEAD)


def solution(mesh):
    rows = P(("grp", "seq"), None)
    return jax.shard_map(
        on_device,
        mesh=mesh,
        in_specs=(rows, rows, rows, rows, P("grp"), P("grp")),
        out_specs=(rows, rows, rows, rows),
        check_vma=False,
    )
```

```python
import math

import jax
import jax.numpy as jnp
from jax import lax
from jax.experimental import pallas as pl
from jax.experimental.pallas import tpu as pltpu
from jax.sharding import PartitionSpec as P

NX = 4
NZ = 8
ROWS = 128
SPAN = 64
HEAD = 128
GROUP = 8
WIDE = GROUP * HEAD
SPANS = 64
REACH = 16
PAD = REACH * SPAN
WINDOW = PAD + SPAN
UNITS = 2 * NX
MESH = pl.DeviceIdType.MESH
SCALE = HEAD ** -0.5
NEG = -1e30
BF = jnp.bfloat16
F32 = jnp.float32


def columns(index, width):
    return pl.ds(pl.multiple_of(index * width, width), width)


def product(a, b, contract):
    return lax.dot_general(a, b, ((contract[0], contract[1]), ((), ())), preferred_element_type=F32)


def hop_count(d, j):
    return NZ // 2 if j == d else NZ // 2 - 1


LANES = [(0, 0), (1, 1), (0, 1), (1, 0)]


def kernel(order_ref, length_ref, q_ref, k_ref, v_ref, g_ref, oo_ref, dqo_ref, dko_ref, dvo_ref,
           qx, gx, kx, vx, kpos, vpos, probs, dkw, dvw, ost, dqst, slot_v, slot_ref,
           outgoing, incoming, mine, total,
           slot_sem, own_in, send_in, recv_in, own_out, send_out, recv_out, own_fin, send_fin, recv_fin,
           gather_send, gather_recv, ring_send, ring_recv):
    me = lax.axis_index("seq")
    x, z = me // NZ, lax.rem(me, NZ)

    def device(xx, zz):
        return {"seq": lax.rem(xx + NX, NX) * NZ + lax.rem(zz + NZ, NZ)}

    barrier = pltpu.get_barrier_semaphore()
    partners = [device(x + d, z) for d in (1, 2, 3)] + [device(x, z + 1), device(x, z - 1)]
    for partner in partners:
        pl.semaphore_signal(barrier, inc=1, device_id=partner, device_id_type=MESH)
    pl.semaphore_wait(barrier, len(partners))

    sources = [k_ref, v_ref, q_ref, g_ref]
    here = pl.ds((z * NX + x) * 2, 2)
    landing = [kx.at[here], vx.at[here], qx.at[x], gx.at[x]]
    widths = [HEAD, HEAD, WIDE, WIDE]
    inward = []

    def outgoing_columns(a, to):
        return sources[a].at[:, :, columns(to, widths[a])] if a < 2 else sources[a].at[:, columns(to, widths[a])]

    for a in range(4):
        row = [pltpu.make_async_copy(outgoing_columns(a, x), landing[a], own_in.at[a])]
        for d in (1, 3, 2):
            to = lax.rem(x + d, NX)
            row.append(pltpu.make_async_remote_copy(
                src_ref=outgoing_columns(a, to),
                dst_ref=landing[a],
                send_sem=send_in.at[a, d - 1],
                recv_sem=recv_in.at[a, d - 1],
                device_id=device(to, z),
                device_id_type=MESH,
            ))
        inward.append(row)
    for a in (0, 1):
        for copy in inward[a]:
            copy.start()
    for d in range(4):
        for a in (2, 3):
            inward[a][d].start()

    def arrived(a, which=range(4)):
        for d in which:
            if d == 0:
                inward[a][0].wait()
            else:
                inward[a][d].wait_recv()

    gathered = [kx, vx]

    def gather_hop(a, d, j, step):
        sign = 1 - 2 * d
        block = gathered[a].at[pl.ds(lax.rem(z - sign * step + NZ, NZ) * 2 * NX + 4 * j, 4)]
        return pltpu.make_async_remote_copy(
            src_ref=block,
            dst_ref=block,
            send_sem=gather_send.at[a, d, j, step],
            recv_sem=gather_recv.at[a, d, j, step],
            device_id=device(x, z + sign),
            device_id_type=MESH,
        )

    def gather_step(a, step):
        for d, j in LANES:
            count = hop_count(d, j)
            if 0 < step <= count:
                gather_hop(a, d, j, step - 1).wait_recv()
            if step < count:
                gather_hop(a, d, j, step).start()

    arrived(0)
    gather_step(0, 0)
    arrived(1)
    def unit_place(i):
        pair, side = i // 2, lax.rem(i, 2)
        near = (pair + 1) // 2 - 2 * (pair // 3)
        away = near * (1 + 2 * side) + 2 * (pair // 3)
        return lax.rem(x + away, NX), near * (pair - 1) + (1 - near) * side

    def unit_span(i):
        xx, half = unit_place(i)
        return order_ref[2 * (xx * NZ + z) + half]

    lane = lax.broadcasted_iota(jnp.int32, (UNITS, HEAD), 1)
    line = lax.broadcasted_iota(jnp.int32, (UNITS, HEAD), 0)

    def find(t, found):
        block = (lax.rem(t // 2, NZ) * NX + t // (2 * NZ)) * 2 + lax.rem(t, 2)
        position = order_ref[t]
        return jnp.where(lane == position, block, found[0]), jnp.where(lane == block, position, found[1])

    nothing = jnp.zeros((UNITS, HEAD), jnp.int32)
    blocks, positions = lax.fori_loop(0, SPANS, find, (nothing, nothing))
    for i in range(UNITS):
        nothing = jnp.where(line == i, unit_span(i), nothing)
    slot_v[0] = blocks
    slot_v[1] = jnp.clip(positions - nothing + REACH + 1, 0, REACH + 2)
    pltpu.make_async_copy(slot_v, slot_ref, slot_sem.at[0]).start()

    def wait_slots():
        pltpu.make_async_copy(slot_v, slot_ref, slot_sem.at[0]).wait()

    kpos[:REACH] = jnp.zeros((REACH, SPAN, HEAD), BF)
    vpos[:REACH] = jnp.zeros((REACH, SPAN, HEAD), BF)
    for unit in range(UNITS):
        dkw[unit, 0] = jnp.zeros((SPAN, HEAD), F32)
        dkw[unit, REACH + 2] = jnp.zeros((SPAN, HEAD), F32)
        dvw[unit, 0] = jnp.zeros((SPAN, HEAD), F32)
        dvw[unit, REACH + 2] = jnp.zeros((SPAN, HEAD), F32)

    gather_step(0, 1)
    gather_step(1, 0)
    gather_step(0, 2)
    gather_step(1, 1)
    gather_step(0, 3)
    gather_step(1, 2)
    gather_step(0, 4)

    def into_positions(source, target):
        @pl.loop(0, SPANS)
        def _(p):
            target[p + REACH] = source[slot_ref[0, 0, p]]

    def window(ref, i):
        c = unit_span(i)
        return jnp.concatenate([ref[c + j] for j in range(REACH + 1)], axis=0)

    def stacked(ref, i):
        xx, half = unit_place(i)
        rows = pl.ds(pl.multiple_of(half * SPAN, SPAN), SPAN)
        return jnp.concatenate([ref[xx, rows, h * HEAD:(h + 1) * HEAD] for h in range(GROUP)], axis=0)

    starts = []
    running = length_ref[0]
    for i in range(1, 8):
        starts.append(running)
        running = running + length_ref[i]

    def weigh(i):
        c = unit_span(i)
        row = c * SPAN + lax.rem(lax.broadcasted_iota(jnp.int32, (1, HEAD), 1), SPAN)
        first = jnp.zeros((1, HEAD), jnp.int32)
        for start in starts:
            first = jnp.where(row >= start, start, first)
        key = (c - REACH) * SPAN + lax.broadcasted_iota(jnp.int32, (WINDOW, HEAD), 0)
        seen = (key >= first) & (key <= row)
        scores = product(window(kpos, i), stacked(qx, i), ((1,), (1,)))
        scores = jnp.where(jnp.concatenate([seen] * (GROUP // 2), axis=1), scores * (SCALE * math.log2(math.e)), NEG)
        weights = jnp.exp2(scores - jnp.max(scores, axis=0, keepdims=True))
        p = (weights * (1.0 / jnp.sum(weights, axis=0, keepdims=True))).astype(BF)
        probs[i] = p
        dvw[i, 1:REACH + 2] = jnp.dot(
            p, stacked(gx, i), preferred_element_type=F32).reshape(REACH + 1, SPAN, HEAD)

    def put_heads(target, i, value_t):
        value = value_t.T
        for h in range(GROUP):
            target[i, :, h * HEAD:(h + 1) * HEAD] = value[h * SPAN:(h + 1) * SPAN]

    staged = [ost, dqst]
    results = [oo_ref, dqo_ref]

    def outward(a, i):
        xx, half = unit_place(i)
        rows = pl.ds(pl.multiple_of(half * SPAN, SPAN), SPAN)
        return pltpu.make_async_remote_copy(
            src_ref=staged[a].at[i],
            dst_ref=results[a].at[rows, columns(x, WIDE)],
            send_sem=send_out.at[a, i - 2],
            recv_sem=recv_out.at[a, i - 2],
            device_id=device(xx, z),
            device_id_type=MESH,
        )

    def keep(a, half):
        rows = pl.ds(half * SPAN, SPAN)
        return pltpu.make_async_copy(
            staged[a].at[half], results[a].at[rows, columns(x, WIDE)], own_out.at[a, half])

    def attend(i):
        q, g, p = stacked(qx, i), stacked(gx, i), probs[i]
        k, v = window(kpos, i), window(vpos, i)
        o_t = product(v, p, ((0,), (0,))).astype(BF)
        delta = jnp.sum(o_t.astype(F32) * g.T.astype(F32), axis=0, keepdims=True)
        slopes = (p.astype(F32) * (product(v, g, ((1,), (1,))) - delta)).astype(BF)
        dkw[i, 1:REACH + 2] = jnp.dot(
            slopes, q, preferred_element_type=F32).reshape(REACH + 1, SPAN, HEAD)
        put_heads(ost, i, o_t)
        put_heads(dqst, i, (product(k, slopes, ((0,), (0,))) * SCALE).astype(BF))

    terms = [dkw, dvw]
    factors = [SCALE, 1.0]

    def ring_hop(a, d, j, step):
        return pltpu.make_async_remote_copy(
            src_ref=outgoing.at[a, d, j, step],
            dst_ref=incoming.at[a, d, j, step],
            send_sem=ring_send.at[a, d, j, step],
            recv_sem=ring_recv.at[a, d, j, step],
            device_id=device(x, z + 1 - 2 * d),
            device_id_type=MESH,
        )

    def own_terms(a, block, j, target):
        @pl.loop(0, 4)
        def _(u):
            value = jnp.zeros((SPAN, HEAD), F32)
            for i in range(UNITS):
                value += terms[a][i, slot_ref[1, i, block * 2 * NX + 4 * j + u]]
            target[u] = value * factors[a]

    def ring_step(a, step):
        lanes = [(d, j) for d, j in LANES if step < hop_count(d, j)]

        def prepare(d, j):
            sign = 1 - 2 * d
            own_terms(a, lax.rem(z + sign * (hop_count(d, j) - step) + NZ, NZ), j, mine.at[d, j])

        if step > 0:
            for d, j in lanes:
                prepare(d, j)
        for d, j in lanes:
            if step == 0:
                prepare(d, j)
            value = mine[d, j]
            if step > 0:
                ring_hop(a, d, j, step - 1).wait_recv()
                value += incoming[a, d, j, step - 1].astype(F32)
            outgoing[a, d, j, step] = value.astype(BF)
            ring_hop(a, d, j, step).start()

    narrow = [dko_ref, dvo_ref]
    finals = []

    def final(a, to, d):
        return pltpu.make_async_remote_copy(
            src_ref=total.at[a, pl.ds(2 * to, 2)],
            dst_ref=narrow[a].at[:, :, columns(x, HEAD)],
            send_sem=send_fin.at[a, d],
            recv_sem=recv_fin.at[a, d],
            device_id=device(to, z),
            device_id_type=MESH,
        )

    def final_own(a):
        return pltpu.make_async_copy(
            total.at[a, pl.ds(2 * x, 2)], narrow[a].at[:, :, columns(x, HEAD)], own_fin.at[a])

    def ring_end(a):
        for j in range(2):
            own_terms(a, z, j, mine.at[0, j])
        for j in range(2):
            value = mine[0, j]
            for d in (1 - j, j):
                last = hop_count(d, j) - 1
                ring_hop(a, d, j, last).wait_recv()
                value += incoming[a, d, j, last].astype(F32)
            total[a, 4 * j:4 * j + 4] = value.astype(BF)
            for d in (2, 1, 3):
                to = lax.rem(x + d, NX)
                pl.when(to // 2 == j)(lambda to=to, d=d: final(a, to, d - 1).start())
            pl.when(x // 2 == j)(lambda: final_own(a).start())

    def take_in(k):
        source = (0, 2, 1, 3)[k]
        arrived(2, (source,))
        arrived(3, (source,))

    def attend_pair(t):
        attend(2 * t)
        attend(2 * t + 1)

    def send_pair(t):
        for half in range(2):
            for a in range(2):
                outward(a, 2 * t + half).start()

    wait_slots()
    into_positions(kx, kpos)

    @pl.loop(0, 2)
    def _(t):
        @pl.when(t == 0)
        def _():
            for k in range(3):
                take_in(k)

        @pl.when(t == 1)
        def _():
            gather_step(1, 3)
            take_in(3)

        for k in range(4):
            weigh(4 * t + k)

    ring_step(1, 0)
    gather_step(1, 4)
    into_positions(vx, vpos)

    @pl.loop(0, NX)
    def _(k):
        pair = 1 + 2 * k - 3 * (k // 2) - 4 * (k // 3)
        for step in (1, 2):
            pl.when(k == step)(lambda step=step: ring_step(1, step))
        attend_pair(pair)
        pl.when(k < 3)(lambda: send_pair(pair))

    for a in range(2):
        for half in range(2):
            keep(a, half).start()
    ring_step(0, 0)
    ring_step(1, 3)
    ring_step(0, 1)
    ring_end(1)
    ring_step(0, 2)
    ring_step(0, 3)
    ring_end(0)

    for row in inward:
        for copy in row[1:]:
            copy.wait_send()
    for a in range(2):
        for d, j in LANES:
            for step in range(hop_count(d, j)):
                gather_hop(a, d, j, step).wait_send()
                ring_hop(a, d, j, step).wait_send()
    for a in range(2):
        for half in range(2):
            keep(a, half).wait()

        @pl.loop(2, UNITS)
        def _(i):
            outward(a, i).wait()

    for a in range(2):
        final_own(a).wait()
        for d in (1, 2, 3):
            final(a, lax.rem(x + d, NX), d - 1).wait()


def hand_over(*refs):
    sources, targets, held = refs[:4], refs[4:8], refs[8:12]
    sem_in, sem_out = refs[12:]
    pieces = [(a, k) for a in range(4) for k in range(4 if a < 2 else 1)]

    def part(ref, a, k):
        size = ROWS // (4 if a < 2 else 1)
        return ref[a].at[pl.ds(k * size, size)]

    def bring(a, k):
        return pltpu.make_async_copy(part(sources, a, k), part(held, a, k), sem_in.at[a, k])

    def give(a, k):
        return pltpu.make_async_copy(part(held, a, k), part(targets, a, k), sem_out.at[a, k])

    for piece in pieces:
        bring(*piece).start()
    for piece in pieces:
        bring(*piece).wait()
        give(*piece).start()
    for piece in pieces:
        give(*piece).wait()


def on_device(queries, keys, values, out_grad, doc_lengths, span_order):
    any_spec = pl.BlockSpec(memory_space=pl.ANY)
    smem = pl.BlockSpec(memory_space=pltpu.SMEM)
    dma = pltpu.SemaphoreType.DMA
    vmem = pltpu.VMEM
    heads = (NX, ROWS, WIDE)
    gathered = (SPANS, SPAN, HEAD)
    padded = (SPANS + REACH, SPAN, HEAD)
    windows = (UNITS, REACH + 3, SPAN, HEAD)
    stage = (UNITS, SPAN, WIDE)
    ring = (2, 2, 2, NZ // 2)
    piece = (4, SPAN, HEAD)
    attended, grad_q, grad_k, grad_v = pl.pallas_call(
        kernel,
        out_shape=[jax.ShapeDtypeStruct((ROWS, NX * WIDE), BF)] * 2 + [
            jax.ShapeDtypeStruct((2, SPAN, NX * HEAD), BF)] * 2,
        in_specs=[smem] * 2 + [any_spec] * 4,
        out_specs=[any_spec] * 4,
        scratch_shapes=[
            vmem(heads, BF), vmem(heads, BF), vmem(gathered, BF), vmem(gathered, BF),
            vmem(padded, BF), vmem(padded, BF), vmem((UNITS, WINDOW, GROUP * SPAN), BF),
            vmem(windows, F32), vmem(windows, F32), vmem(stage, BF), vmem(stage, BF),
            vmem((2, UNITS, HEAD), jnp.int32), pltpu.SMEM((2, UNITS, HEAD), jnp.int32),
            vmem(ring + piece, BF), vmem(ring + piece, BF), vmem((2, 2) + piece, F32), vmem((2, UNITS, SPAN, HEAD), BF),
            dma((1,)), dma((4,)), dma((4, 3)), dma((4, 3)),
            dma((2, 2)), dma((2, UNITS - 2)), dma((2, UNITS - 2)),
            dma((2,)), dma((2, 3)), dma((2, 3)),
            dma(ring), dma(ring), dma(ring), dma(ring),
        ],
        compiler_params=pltpu.CompilerParams(
            collective_id=0, has_side_effects=True, vmem_limit_bytes=56 * 2 ** 20),
        name="attention",
    )(span_order, doc_lengths, queries, keys.reshape(2, SPAN, NX * HEAD), values.reshape(2, SPAN, NX * HEAD), out_grad)
    results = (attended, grad_q, grad_k.reshape(ROWS, NX * HEAD), grad_v.reshape(ROWS, NX * HEAD))
    return pl.pallas_call(
        hand_over,
        out_shape=[jax.ShapeDtypeStruct(result.shape, BF) for result in results],
        in_specs=[any_spec] * 4,
        out_specs=[any_spec] * 4,
        scratch_shapes=[vmem(result.shape, BF) for result in results] + [dma((4, 4)), dma((4, 4))],
        name="hand_over",
    )(*results)


def solution(mesh):
    rows = P(("grp", "seq"), None)
    return jax.shard_map(
        lambda *args: tuple(on_device(*args)),
        mesh=mesh,
        in_specs=(rows, rows, rows, rows, P("grp"), P("grp")),
        out_specs=(rows, rows, rows, rows),
        check_vma=False,
    )
```

```python
import math

import jax
import jax.numpy as jnp
from jax import lax
from jax.experimental import pallas as pl
from jax.experimental.pallas import tpu as pltpu
from jax.sharding import PartitionSpec as P

NX = 4
NZ = 8
ROWS = 128
SPAN = 64
HEAD = 128
GROUP = 8
WIDE = GROUP * HEAD
SPANS = 64
REACH = 16
PAD = REACH * SPAN
WINDOW = PAD + SPAN
UNITS = 2 * NX
MESH = pl.DeviceIdType.MESH
SCALE = HEAD ** -0.5
NEG = -1e30
BF = jnp.bfloat16
F32 = jnp.float32


def columns(index, width):
    return pl.ds(pl.multiple_of(index * width, width), width)


def product(a, b, contract):
    return lax.dot_general(a, b, ((contract[0], contract[1]), ((), ())), preferred_element_type=F32)


def hop_count(d, j):
    return NZ // 2 if j == d else NZ // 2 - 1


LANES = [(0, 0), (1, 1), (0, 1), (1, 0)]


def kernel(order_ref, length_ref, q_ref, k_ref, v_ref, g_ref, oo_ref, dqo_ref, dko_ref, dvo_ref,
           qx, gx, kx, vx, kpos, vpos, probs, dkw, dvw, ost, dqst, slot_v, slot_ref,
           outgoing, incoming, mine, total,
           slot_sem, own_in, send_in, recv_in, own_out, send_out, recv_out, own_fin, send_fin, recv_fin,
           gather_send, gather_recv, ring_send, ring_recv):
    me = lax.axis_index("seq")
    x, z = me // NZ, lax.rem(me, NZ)

    def device(xx, zz):
        return {"seq": lax.rem(xx + NX, NX) * NZ + lax.rem(zz + NZ, NZ)}

    barrier = pltpu.get_barrier_semaphore()
    partners = [device(x + d, z) for d in (1, 2, 3)] + [device(x, z + 1), device(x, z - 1)]
    for partner in partners:
        pl.semaphore_signal(barrier, inc=1, device_id=partner, device_id_type=MESH)
    pl.semaphore_wait(barrier, len(partners))

    sources = [k_ref, v_ref, q_ref, g_ref]
    here = pl.ds((z * NX + x) * 2, 2)
    landing = [kx.at[here], vx.at[here], qx.at[x], gx.at[x]]
    widths = [HEAD, HEAD, WIDE, WIDE]
    inward = []

    def outgoing_columns(a, to):
        return sources[a].at[:, :, columns(to, widths[a])] if a < 2 else sources[a].at[:, columns(to, widths[a])]

    for a in range(4):
        row = [pltpu.make_async_copy(outgoing_columns(a, x), landing[a], own_in.at[a])]
        for d in (1, 3, 2):
            to = lax.rem(x + d, NX)
            row.append(pltpu.make_async_remote_copy(
                src_ref=outgoing_columns(a, to),
                dst_ref=landing[a],
                send_sem=send_in.at[a, d - 1],
                recv_sem=recv_in.at[a, d - 1],
                device_id=device(to, z),
                device_id_type=MESH,
            ))
        inward.append(row)
    for a in (0, 1):
        for copy in inward[a]:
            copy.start()
    for d in range(4):
        for a in (2, 3):
            inward[a][d].start()

    def arrived(a, which=range(4)):
        for d in which:
            if d == 0:
                inward[a][0].wait()
            else:
                inward[a][d].wait_recv()

    gathered = [kx, vx]

    def gather_hop(a, d, j, step):
        sign = 1 - 2 * d
        block = gathered[a].at[pl.ds(lax.rem(z - sign * step + NZ, NZ) * 2 * NX + 4 * j, 4)]
        return pltpu.make_async_remote_copy(
            src_ref=block,
            dst_ref=block,
            send_sem=gather_send.at[a, d, j, step],
            recv_sem=gather_recv.at[a, d, j, step],
            device_id=device(x, z + sign),
            device_id_type=MESH,
        )

    def gather_step(a, step):
        for d, j in LANES:
            count = hop_count(d, j)
            if 0 < step <= count:
                gather_hop(a, d, j, step - 1).wait_recv()
            if step < count:
                gather_hop(a, d, j, step).start()

    arrived(0)
    gather_step(0, 0)
    arrived(1)
    def unit_place(i):
        pair, side = i // 2, lax.rem(i, 2)
        near = (pair + 1) // 2 - 2 * (pair // 3)
        away = near * (1 + 2 * side) + 2 * (pair // 3)
        return lax.rem(x + away, NX), near * (pair - 1) + (1 - near) * side

    def unit_span(i):
        xx, half = unit_place(i)
        return order_ref[2 * (xx * NZ + z) + half]

    lane = lax.broadcasted_iota(jnp.int32, (UNITS, HEAD), 1)
    line = lax.broadcasted_iota(jnp.int32, (UNITS, HEAD), 0)

    def find(t, found):
        block = (lax.rem(t // 2, NZ) * NX + t // (2 * NZ)) * 2 + lax.rem(t, 2)
        position = order_ref[t]
        return jnp.where(lane == position, block, found[0]), jnp.where(lane == block, position, found[1])

    nothing = jnp.zeros((UNITS, HEAD), jnp.int32)
    blocks, positions = lax.fori_loop(0, SPANS, find, (nothing, nothing))
    for i in range(UNITS):
        nothing = jnp.where(line == i, unit_span(i), nothing)
    slot_v[0] = blocks
    slot_v[1] = jnp.clip(positions - nothing + REACH + 1, 0, REACH + 2)
    pltpu.make_async_copy(slot_v, slot_ref, slot_sem.at[0]).start()

    def wait_slots():
        pltpu.make_async_copy(slot_v, slot_ref, slot_sem.at[0]).wait()

    kpos[:REACH] = jnp.zeros((REACH, SPAN, HEAD), BF)
    vpos[:REACH] = jnp.zeros((REACH, SPAN, HEAD), BF)
    for unit in range(UNITS):
        dkw[unit, 0] = jnp.zeros((SPAN, HEAD), F32)
        dkw[unit, REACH + 2] = jnp.zeros((SPAN, HEAD), F32)
        dvw[unit, 0] = jnp.zeros((SPAN, HEAD), F32)
        dvw[unit, REACH + 2] = jnp.zeros((SPAN, HEAD), F32)

    gather_step(0, 1)
    gather_step(1, 0)
    gather_step(0, 2)
    gather_step(1, 1)
    gather_step(0, 3)
    gather_step(1, 2)
    gather_step(0, 4)

    def into_positions(source, target):
        @pl.loop(0, SPANS)
        def _(p):
            target[p + REACH] = source[slot_ref[0, 0, p]]

    def window(ref, i):
        c = unit_span(i)
        return jnp.concatenate([ref[c + j] for j in range(REACH + 1)], axis=0)

    def stacked(ref, i):
        xx, half = unit_place(i)
        rows = pl.ds(pl.multiple_of(half * SPAN, SPAN), SPAN)
        return jnp.concatenate([ref[xx, rows, h * HEAD:(h + 1) * HEAD] for h in range(GROUP)], axis=0)

    starts = []
    running = length_ref[0]
    for i in range(1, 8):
        starts.append(running)
        running = running + length_ref[i]

    def weigh(i):
        c = unit_span(i)
        row = c * SPAN + lax.rem(lax.broadcasted_iota(jnp.int32, (1, HEAD), 1), SPAN)
        first = jnp.zeros((1, HEAD), jnp.int32)
        for start in starts:
            first = jnp.where(row >= start, start, first)
        key = (c - REACH) * SPAN + lax.broadcasted_iota(jnp.int32, (WINDOW, HEAD), 0)
        seen = (key >= first) & (key <= row)
        scores = product(window(kpos, i), stacked(qx, i), ((1,), (1,)))
        scores = jnp.where(jnp.concatenate([seen] * (GROUP // 2), axis=1), scores * (SCALE * math.log2(math.e)), NEG)
        weights = jnp.exp2(scores - jnp.max(scores, axis=0, keepdims=True))
        p = (weights * (1.0 / jnp.sum(weights, axis=0, keepdims=True))).astype(BF)
        probs[i] = p
        dvw[i, 1:REACH + 2] = jnp.dot(
            p, stacked(gx, i), preferred_element_type=F32).reshape(REACH + 1, SPAN, HEAD)

    def put_heads(target, i, value_t):
        value = value_t.T
        for h in range(GROUP):
            target[i, :, h * HEAD:(h + 1) * HEAD] = value[h * SPAN:(h + 1) * SPAN]

    staged = [ost, dqst]
    results = [oo_ref, dqo_ref]

    def outward(a, i):
        xx, half = unit_place(i)
        rows = pl.ds(pl.multiple_of(half * SPAN, SPAN), SPAN)
        return pltpu.make_async_remote_copy(
            src_ref=staged[a].at[i],
            dst_ref=results[a].at[rows, columns(x, WIDE)],
            send_sem=send_out.at[a, i - 2],
            recv_sem=recv_out.at[a, i - 2],
            device_id=device(xx, z),
            device_id_type=MESH,
        )

    def keep(a, half):
        rows = pl.ds(half * SPAN, SPAN)
        return pltpu.make_async_copy(
            staged[a].at[half], results[a].at[rows, columns(x, WIDE)], own_out.at[a, half])

    def attend(i):
        q, g, p = stacked(qx, i), stacked(gx, i), probs[i]
        v = window(vpos, i)
        o_t = product(v, p, ((0,), (0,))).astype(BF)
        delta = jnp.sum(o_t.astype(F32) * g.T.astype(F32), axis=0, keepdims=True)
        slopes = (p.astype(F32) * (product(v, g, ((1,), (1,))) - delta)).astype(BF)
        dkw[i, 1:REACH + 2] = jnp.dot(
            slopes, q, preferred_element_type=F32).reshape(REACH + 1, SPAN, HEAD)
        probs[i] = slopes
        put_heads(ost, i, o_t)

    def query_grad(i):
        put_heads(dqst, i, (product(window(kpos, i), probs[i], ((0,), (0,))) * SCALE).astype(BF))

    terms = [dkw, dvw]
    factors = [SCALE, 1.0]

    def ring_hop(a, d, j, step):
        return pltpu.make_async_remote_copy(
            src_ref=outgoing.at[a, d, j, step],
            dst_ref=incoming.at[a, d, j, step],
            send_sem=ring_send.at[a, d, j, step],
            recv_sem=ring_recv.at[a, d, j, step],
            device_id=device(x, z + 1 - 2 * d),
            device_id_type=MESH,
        )

    def own_terms(a, block, j, target):
        @pl.loop(0, 4)
        def _(u):
            value = jnp.zeros((SPAN, HEAD), F32)
            for i in range(UNITS):
                value += terms[a][i, slot_ref[1, i, block * 2 * NX + 4 * j + u]]
            target[u] = value * factors[a]

    def ring_step(a, step):
        lanes = [(d, j) for d, j in LANES if step < hop_count(d, j)]

        def prepare(d, j):
            sign = 1 - 2 * d
            own_terms(a, lax.rem(z + sign * (hop_count(d, j) - step) + NZ, NZ), j, mine.at[d, j])

        if step > 0:
            for d, j in lanes:
                prepare(d, j)
        for d, j in lanes:
            if step == 0:
                prepare(d, j)
            value = mine[d, j]
            if step > 0:
                ring_hop(a, d, j, step - 1).wait_recv()
                value += incoming[a, d, j, step - 1].astype(F32)
            outgoing[a, d, j, step] = value.astype(BF)
            ring_hop(a, d, j, step).start()

    narrow = [dko_ref, dvo_ref]
    finals = []

    def final(a, to, d):
        return pltpu.make_async_remote_copy(
            src_ref=total.at[a, pl.ds(2 * to, 2)],
            dst_ref=narrow[a].at[:, :, columns(x, HEAD)],
            send_sem=send_fin.at[a, d],
            recv_sem=recv_fin.at[a, d],
            device_id=device(to, z),
            device_id_type=MESH,
        )

    def final_own(a):
        return pltpu.make_async_copy(
            total.at[a, pl.ds(2 * x, 2)], narrow[a].at[:, :, columns(x, HEAD)], own_fin.at[a])

    def ring_end(a):
        for j in range(2):
            own_terms(a, z, j, mine.at[0, j])
        for j in range(2):
            value = mine[0, j]
            for d in (1 - j, j):
                last = hop_count(d, j) - 1
                ring_hop(a, d, j, last).wait_recv()
                value += incoming[a, d, j, last].astype(F32)
            total[a, 4 * j:4 * j + 4] = value.astype(BF)
            for d in (2, 1, 3):
                to = lax.rem(x + d, NX)
                pl.when(to // 2 == j)(lambda to=to, d=d: final(a, to, d - 1).start())
            pl.when(x // 2 == j)(lambda: final_own(a).start())

    def take_in(k):
        source = (0, 2, 1, 3)[k]
        arrived(2, (source,))
        arrived(3, (source,))

    def each_pair(a, body, begin, end, beside=None):
        @pl.loop(begin, end)
        def _(k):
            pair = 1 + 2 * k - 3 * (k // 2) - 4 * (k // 3)
            if beside is not None:
                beside(k)
            body(2 * pair)
            body(2 * pair + 1)

            @pl.when(k < 3)
            def _():
                for side in range(2):
                    outward(a, 2 * pair + side).start()

    wait_slots()
    into_positions(kx, kpos)

    @pl.loop(0, 2)
    def _(t):
        @pl.when(t == 0)
        def _():
            for k in range(3):
                take_in(k)

        @pl.when(t == 1)
        def _():
            gather_step(1, 3)
            take_in(3)

        for k in range(4):
            weigh(4 * t + k)

    ring_step(1, 0)
    gather_step(1, 4)
    into_positions(vx, vpos)

    def beside(k):
        pl.when(k == 1)(lambda: ring_step(1, 1))
        pl.when(k == 3)(lambda: ring_step(1, 2))

    each_pair(0, attend, 0, 4, beside)
    ring_step(0, 0)

    def beside_query(k):
        pl.when(k == 1)(lambda: ring_step(1, 3))
        pl.when(k == 3)(lambda: ring_step(0, 1))

    each_pair(1, query_grad, 0, 4, beside_query)
    for a in range(2):
        for half in range(2):
            keep(a, half).start()
    ring_end(1)
    ring_step(0, 2)
    ring_step(0, 3)
    ring_end(0)

    for row in inward:
        for copy in row[1:]:
            copy.wait_send()
    for a in range(2):
        for d, j in LANES:
            for step in range(hop_count(d, j)):
                gather_hop(a, d, j, step).wait_send()
                ring_hop(a, d, j, step).wait_send()
    for a in range(2):
        for half in range(2):
            keep(a, half).wait()

        @pl.loop(2, UNITS)
        def _(i):
            outward(a, i).wait()

    for a in range(2):
        final_own(a).wait()
        for d in (1, 2, 3):
            final(a, lax.rem(x + d, NX), d - 1).wait()


def hand_over(*refs):
    sources, targets, held = refs[:4], refs[4:8], refs[8:12]
    sem_in, sem_out = refs[12:]
    pieces = [(a, k) for a in range(4) for k in range(4 if a < 2 else 1)]

    def part(ref, a, k):
        size = ROWS // (4 if a < 2 else 1)
        return ref[a].at[pl.ds(k * size, size)]

    def bring(a, k):
        return pltpu.make_async_copy(part(sources, a, k), part(held, a, k), sem_in.at[a, k])

    def give(a, k):
        return pltpu.make_async_copy(part(held, a, k), part(targets, a, k), sem_out.at[a, k])

    for piece in pieces:
        bring(*piece).start()
    for piece in pieces:
        bring(*piece).wait()
        give(*piece).start()
    for piece in pieces:
        give(*piece).wait()


def on_device(queries, keys, values, out_grad, doc_lengths, span_order):
    any_spec = pl.BlockSpec(memory_space=pl.ANY)
    smem = pl.BlockSpec(memory_space=pltpu.SMEM)
    dma = pltpu.SemaphoreType.DMA
    vmem = pltpu.VMEM
    heads = (NX, ROWS, WIDE)
    gathered = (SPANS, SPAN, HEAD)
    padded = (SPANS + REACH, SPAN, HEAD)
    windows = (UNITS, REACH + 3, SPAN, HEAD)
    stage = (UNITS, SPAN, WIDE)
    ring = (2, 2, 2, NZ // 2)
    piece = (4, SPAN, HEAD)
    attended, grad_q, grad_k, grad_v = pl.pallas_call(
        kernel,
        out_shape=[jax.ShapeDtypeStruct((ROWS, NX * WIDE), BF)] * 2 + [
            jax.ShapeDtypeStruct((2, SPAN, NX * HEAD), BF)] * 2,
        in_specs=[smem] * 2 + [any_spec] * 4,
        out_specs=[any_spec] * 4,
        scratch_shapes=[
            vmem(heads, BF), vmem(heads, BF), vmem(gathered, BF), vmem(gathered, BF),
            vmem(padded, BF), vmem(padded, BF), vmem((UNITS, WINDOW, GROUP * SPAN), BF),
            vmem(windows, F32), vmem(windows, F32), vmem(stage, BF), vmem(stage, BF),
            vmem((2, UNITS, HEAD), jnp.int32), pltpu.SMEM((2, UNITS, HEAD), jnp.int32),
            vmem(ring + piece, BF), vmem(ring + piece, BF), vmem((2, 2) + piece, F32), vmem((2, UNITS, SPAN, HEAD), BF),
            dma((1,)), dma((4,)), dma((4, 3)), dma((4, 3)),
            dma((2, 2)), dma((2, UNITS - 2)), dma((2, UNITS - 2)),
            dma((2,)), dma((2, 3)), dma((2, 3)),
            dma(ring), dma(ring), dma(ring), dma(ring),
        ],
        compiler_params=pltpu.CompilerParams(
            collective_id=0, has_side_effects=True, vmem_limit_bytes=56 * 2 ** 20),
        name="attention",
    )(span_order, doc_lengths, queries, keys.reshape(2, SPAN, NX * HEAD), values.reshape(2, SPAN, NX * HEAD), out_grad)
    results = (attended, grad_q, grad_k.reshape(ROWS, NX * HEAD), grad_v.reshape(ROWS, NX * HEAD))
    return pl.pallas_call(
        hand_over,
        out_shape=[jax.ShapeDtypeStruct(result.shape, BF) for result in results],
        in_specs=[any_spec] * 4,
        out_specs=[any_spec] * 4,
        scratch_shapes=[vmem(result.shape, BF) for result in results] + [dma((4, 4)), dma((4, 4))],
        name="hand_over",
    )(*results)


def solution(mesh):
    rows = P(("grp", "seq"), None)
    return jax.shard_map(
        lambda *args: tuple(on_device(*args)),
        mesh=mesh,
        in_specs=(rows, rows, rows, rows, P("grp"), P("grp")),
        out_specs=(rows, rows, rows, rows),
        check_vma=False,
    )
```

```python
import math

import jax
import jax.numpy as jnp
from jax import lax
from jax.experimental import pallas as pl
from jax.experimental.pallas import tpu as pltpu
from jax.sharding import PartitionSpec as P

NX = 4
NZ = 8
ROWS = 128
SPAN = 64
HEAD = 128
GROUP = 8
WIDE = GROUP * HEAD
SPANS = 64
REACH = 16
PAD = REACH * SPAN
WINDOW = PAD + SPAN
UNITS = 2 * NX
MESH = pl.DeviceIdType.MESH
SCALE = HEAD ** -0.5
NEG = -1e30
BF = jnp.bfloat16
F32 = jnp.float32


def columns(index, width):
    return pl.ds(pl.multiple_of(index * width, width), width)


def product(a, b, contract):
    return lax.dot_general(a, b, ((contract[0], contract[1]), ((), ())), preferred_element_type=F32)


def hop_count(d, j):
    return NZ // 2 if j == d else NZ // 2 - 1


LANES = [(0, 0), (1, 1), (0, 1), (1, 0)]


def kernel(order_ref, length_ref, q_ref, k_ref, v_ref, g_ref, oo_ref, dqo_ref, dko_ref, dvo_ref,
           qx, gx, kx, vx, kpos, vpos, probs, dkw, dvw, ost, dqst, slot_v, slot_ref,
           outgoing, incoming, mine, total,
           slot_sem, own_in, send_in, recv_in, own_out, send_out, recv_out, own_fin, send_fin, recv_fin,
           gather_send, gather_recv, ring_send, ring_recv):
    me = lax.axis_index("seq")
    x, z = me // NZ, lax.rem(me, NZ)

    def device(xx, zz):
        return {"seq": lax.rem(xx + NX, NX) * NZ + lax.rem(zz + NZ, NZ)}

    barrier = pltpu.get_barrier_semaphore()
    partners = [device(x + d, z) for d in (1, 2, 3)] + [device(x, z + 1), device(x, z - 1)]
    for partner in partners:
        pl.semaphore_signal(barrier, inc=1, device_id=partner, device_id_type=MESH)
    pl.semaphore_wait(barrier, len(partners))

    sources = [k_ref, v_ref, q_ref, g_ref]
    here = pl.ds((z * NX + x) * 2, 2)
    landing = [kx.at[here], vx.at[here], qx.at[x], gx.at[x]]
    widths = [HEAD, HEAD, WIDE, WIDE]
    inward = []

    def outgoing_columns(a, to):
        return sources[a].at[:, :, columns(to, widths[a])] if a < 2 else sources[a].at[:, columns(to, widths[a])]

    for a in range(4):
        row = [pltpu.make_async_copy(outgoing_columns(a, x), landing[a], own_in.at[a])]
        for d in (1, 3, 2):
            to = lax.rem(x + d, NX)
            row.append(pltpu.make_async_remote_copy(
                src_ref=outgoing_columns(a, to),
                dst_ref=landing[a],
                send_sem=send_in.at[a, d - 1],
                recv_sem=recv_in.at[a, d - 1],
                device_id=device(to, z),
                device_id_type=MESH,
            ))
        inward.append(row)
    for a in (0, 1):
        for copy in inward[a]:
            copy.start()
    for d in range(4):
        for a in (2, 3):
            inward[a][d].start()

    def arrived(a, which=range(4)):
        for d in which:
            if d == 0:
                inward[a][0].wait()
            else:
                inward[a][d].wait_recv()

    gathered = [kx, vx]

    def gather_hop(a, d, j, step):
        sign = 1 - 2 * d
        block = gathered[a].at[pl.ds(lax.rem(z - sign * step + NZ, NZ) * 2 * NX + 4 * j, 4)]
        return pltpu.make_async_remote_copy(
            src_ref=block,
            dst_ref=block,
            send_sem=gather_send.at[a, d, j, step],
            recv_sem=gather_recv.at[a, d, j, step],
            device_id=device(x, z + sign),
            device_id_type=MESH,
        )

    def gather_step(a, step):
        for d, j in LANES:
            count = hop_count(d, j)
            if 0 < step <= count:
                gather_hop(a, d, j, step - 1).wait_recv()
            if step < count:
                gather_hop(a, d, j, step).start()

    def unit_place(i):
        pair, side = i // 2, lax.rem(i, 2)
        near = (pair + 1) // 2 - 2 * (pair // 3)
        away = near * (1 + 2 * side) + 2 * (pair // 3)
        return lax.rem(x + away, NX), near * (pair - 1) + (1 - near) * side

    def unit_span(i):
        xx, half = unit_place(i)
        return order_ref[2 * (xx * NZ + z) + half]

    lane = lax.broadcasted_iota(jnp.int32, (UNITS, HEAD), 1)
    line = lax.broadcasted_iota(jnp.int32, (UNITS, HEAD), 0)

    def find(t, found):
        block = (lax.rem(t // 2, NZ) * NX + t // (2 * NZ)) * 2 + lax.rem(t, 2)
        position = order_ref[t]
        return jnp.where(lane == position, block, found[0]), jnp.where(lane == block, position, found[1])

    nothing = jnp.zeros((UNITS, HEAD), jnp.int32)
    blocks, positions = lax.fori_loop(0, SPANS, find, (nothing, nothing))
    for i in range(UNITS):
        nothing = jnp.where(line == i, unit_span(i), nothing)
    slot_v[0] = blocks
    slot_v[1] = jnp.clip(positions - nothing + REACH + 1, 0, REACH + 2)
    pltpu.make_async_copy(slot_v, slot_ref, slot_sem.at[0]).start()

    def wait_slots():
        pltpu.make_async_copy(slot_v, slot_ref, slot_sem.at[0]).wait()

    kpos[:REACH] = jnp.zeros((REACH, SPAN, HEAD), BF)
    vpos[:REACH] = jnp.zeros((REACH, SPAN, HEAD), BF)
    for unit in range(UNITS):
        dkw[unit, 0] = jnp.zeros((SPAN, HEAD), F32)
        dkw[unit, REACH + 2] = jnp.zeros((SPAN, HEAD), F32)
        dvw[unit, 0] = jnp.zeros((SPAN, HEAD), F32)
        dvw[unit, REACH + 2] = jnp.zeros((SPAN, HEAD), F32)

    arrived(0)
    gather_step(0, 0)
    gather_step(0, 1)
    arrived(1)
    gather_step(1, 0)
    gather_step(0, 2)
    gather_step(1, 1)
    gather_step(0, 3)
    gather_step(1, 2)
    gather_step(0, 4)

    def into_positions(source, target):
        @pl.loop(0, SPANS)
        def _(p):
            target[p + REACH] = source[slot_ref[0, 0, p]]

    def window(ref, i):
        c = unit_span(i)
        return jnp.concatenate([ref[c + j] for j in range(REACH + 1)], axis=0)

    def stacked(ref, i):
        xx, half = unit_place(i)
        rows = pl.ds(pl.multiple_of(half * SPAN, SPAN), SPAN)
        return jnp.concatenate([ref[xx, rows, h * HEAD:(h + 1) * HEAD] for h in range(GROUP)], axis=0)

    starts = []
    running = length_ref[0]
    for i in range(1, 8):
        starts.append(running)
        running = running + length_ref[i]

    def weigh(i):
        c = unit_span(i)
        row = c * SPAN + lax.rem(lax.broadcasted_iota(jnp.int32, (1, HEAD), 1), SPAN)
        first = jnp.zeros((1, HEAD), jnp.int32)
        for start in starts:
            first = jnp.where(row >= start, start, first)
        key = (c - REACH) * SPAN + lax.broadcasted_iota(jnp.int32, (WINDOW, HEAD), 0)
        seen = (key >= first) & (key <= row)
        scores = product(window(kpos, i), stacked(qx, i), ((1,), (1,)))
        scores = jnp.where(jnp.concatenate([seen] * (GROUP // 2), axis=1), scores * (SCALE * math.log2(math.e)), NEG)
        weights = jnp.exp2(scores - jnp.max(scores, axis=0, keepdims=True))
        p = (weights * (1.0 / jnp.sum(weights, axis=0, keepdims=True))).astype(BF)
        probs[i] = p
        dvw[i, 1:REACH + 2] = jnp.dot(
            p, stacked(gx, i), preferred_element_type=F32).reshape(REACH + 1, SPAN, HEAD)

    def put_heads(target, i, value_t):
        value = value_t.T
        for h in range(GROUP):
            target[i, :, h * HEAD:(h + 1) * HEAD] = value[h * SPAN:(h + 1) * SPAN]

    staged = [ost, dqst]
    results = [oo_ref, dqo_ref]

    def outward(a, i):
        xx, half = unit_place(i)
        rows = pl.ds(pl.multiple_of(half * SPAN, SPAN), SPAN)
        return pltpu.make_async_remote_copy(
            src_ref=staged[a].at[i],
            dst_ref=results[a].at[rows, columns(x, WIDE)],
            send_sem=send_out.at[a, i - 2],
            recv_sem=recv_out.at[a, i - 2],
            device_id=device(xx, z),
            device_id_type=MESH,
        )

    def keep(a, half):
        rows = pl.ds(half * SPAN, SPAN)
        return pltpu.make_async_copy(
            staged[a].at[half], results[a].at[rows, columns(x, WIDE)], own_out.at[a, half])

    def attend(i):
        q, g, p = stacked(qx, i), stacked(gx, i), probs[i]
        v = window(vpos, i)
        o_t = product(v, p, ((0,), (0,))).astype(BF)
        delta = jnp.sum(o_t.astype(F32) * g.T.astype(F32), axis=0, keepdims=True)
        slopes = (p.astype(F32) * (product(v, g, ((1,), (1,))) - delta)).astype(BF)
        dkw[i, 1:REACH + 2] = jnp.dot(
            slopes, q, preferred_element_type=F32).reshape(REACH + 1, SPAN, HEAD)
        probs[i] = slopes
        put_heads(ost, i, o_t)

    def query_grad(i):
        put_heads(dqst, i, (product(window(kpos, i), probs[i], ((0,), (0,))) * SCALE).astype(BF))

    terms = [dkw, dvw]
    factors = [SCALE, 1.0]

    def ring_hop(a, d, j, step):
        return pltpu.make_async_remote_copy(
            src_ref=outgoing.at[a, d, j, step],
            dst_ref=incoming.at[a, d, j, step],
            send_sem=ring_send.at[a, d, j, step],
            recv_sem=ring_recv.at[a, d, j, step],
            device_id=device(x, z + 1 - 2 * d),
            device_id_type=MESH,
        )

    def own_terms(a, block, j, target):
        @pl.loop(0, 4)
        def _(u):
            value = jnp.zeros((SPAN, HEAD), F32)
            for i in range(UNITS):
                value += terms[a][i, slot_ref[1, i, block * 2 * NX + 4 * j + u]]
            target[u] = value * factors[a]

    def ring_step(a, step):
        lanes = [(d, j) for d, j in LANES if step < hop_count(d, j)]

        def prepare(d, j):
            sign = 1 - 2 * d
            own_terms(a, lax.rem(z + sign * (hop_count(d, j) - step) + NZ, NZ), j, mine.at[d, j])

        if step > 0:
            for d, j in lanes:
                prepare(d, j)
        for d, j in lanes:
            if step == 0:
                prepare(d, j)
            value = mine[d, j]
            if step > 0:
                ring_hop(a, d, j, step - 1).wait_recv()
                value += incoming[a, d, j, step - 1].astype(F32)
            outgoing[a, d, j, step] = value.astype(BF)
            ring_hop(a, d, j, step).start()

    narrow = [dko_ref, dvo_ref]
    finals = []

    def final(a, to, d):
        return pltpu.make_async_remote_copy(
            src_ref=total.at[a, pl.ds(2 * to, 2)],
            dst_ref=narrow[a].at[:, :, columns(x, HEAD)],
            send_sem=send_fin.at[a, d],
            recv_sem=recv_fin.at[a, d],
            device_id=device(to, z),
            device_id_type=MESH,
        )

    def final_own(a):
        return pltpu.make_async_copy(
            total.at[a, pl.ds(2 * x, 2)], narrow[a].at[:, :, columns(x, HEAD)], own_fin.at[a])

    def ring_end(a):
        for j in range(2):
            own_terms(a, z, j, mine.at[0, j])
        for j in range(2):
            value = mine[0, j]
            for d in (1 - j, j):
                last = hop_count(d, j) - 1
                ring_hop(a, d, j, last).wait_recv()
                value += incoming[a, d, j, last].astype(F32)
            total[a, 4 * j:4 * j + 4] = value.astype(BF)
            for d in (2, 1, 3):
                to = lax.rem(x + d, NX)
                pl.when(to // 2 == j)(lambda to=to, d=d: final(a, to, d - 1).start())
            pl.when(x // 2 == j)(lambda: final_own(a).start())

    def take_in(k):
        source = (0, 2, 1, 3)[k]
        arrived(2, (source,))
        arrived(3, (source,))

    def each_pair(a, body, begin, end, beside=None):
        @pl.loop(begin, end)
        def _(k):
            pair = 1 + 2 * k - 3 * (k // 2) - 4 * (k // 3)
            if beside is not None:
                beside(k)
            body(2 * pair)
            body(2 * pair + 1)

            @pl.when(k < 3)
            def _():
                for side in range(2):
                    outward(a, 2 * pair + side).start()

    wait_slots()
    into_positions(kx, kpos)

    @pl.loop(0, 2)
    def _(t):
        @pl.when(t == 0)
        def _():
            for k in range(3):
                take_in(k)

        @pl.when(t == 1)
        def _():
            gather_step(1, 3)
            take_in(3)

        for k in range(4):
            weigh(4 * t + k)

    ring_step(1, 0)
    gather_step(1, 4)
    into_positions(vx, vpos)

    def beside(k):
        pl.when(k == 1)(lambda: ring_step(1, 1))
        pl.when(k == 3)(lambda: ring_step(1, 2))

    each_pair(0, attend, 0, 4, beside)
    ring_step(0, 0)

    def beside_query(k):
        pl.when(k == 1)(lambda: ring_step(1, 3))
        pl.when(k == 3)(lambda: ring_step(0, 1))

    each_pair(1, query_grad, 0, 4, beside_query)
    for a in range(2):
        for half in range(2):
            keep(a, half).start()
    ring_end(1)
    ring_step(0, 2)
    ring_step(0, 3)
    ring_end(0)

    for row in inward:
        for copy in row[1:]:
            copy.wait_send()
    for a in range(2):
        for d, j in LANES:
            for step in range(hop_count(d, j)):
                gather_hop(a, d, j, step).wait_send()
                ring_hop(a, d, j, step).wait_send()
    for a in range(2):
        for half in range(2):
            keep(a, half).wait()

        @pl.loop(2, UNITS)
        def _(i):
            outward(a, i).wait()

    for a in range(2):
        final_own(a).wait()
        for d in (1, 2, 3):
            final(a, lax.rem(x + d, NX), d - 1).wait()


def hand_over(*refs):
    sources, targets, held = refs[:4], refs[4:8], refs[8:12]
    sem_in, sem_out = refs[12:]
    pieces = [(a, k) for a in range(4) for k in range(4 if a < 2 else 1)]

    def part(ref, a, k):
        size = ROWS // (4 if a < 2 else 1)
        return ref[a].at[pl.ds(k * size, size)]

    def bring(a, k):
        return pltpu.make_async_copy(part(sources, a, k), part(held, a, k), sem_in.at[a, k])

    def give(a, k):
        return pltpu.make_async_copy(part(held, a, k), part(targets, a, k), sem_out.at[a, k])

    for piece in pieces:
        bring(*piece).start()
    for piece in pieces:
        bring(*piece).wait()
        give(*piece).start()
    for piece in pieces:
        give(*piece).wait()


def on_device(queries, keys, values, out_grad, doc_lengths, span_order):
    any_spec = pl.BlockSpec(memory_space=pl.ANY)
    smem = pl.BlockSpec(memory_space=pltpu.SMEM)
    dma = pltpu.SemaphoreType.DMA
    vmem = pltpu.VMEM
    heads = (NX, ROWS, WIDE)
    gathered = (SPANS, SPAN, HEAD)
    padded = (SPANS + REACH, SPAN, HEAD)
    windows = (UNITS, REACH + 3, SPAN, HEAD)
    stage = (UNITS, SPAN, WIDE)
    ring = (2, 2, 2, NZ // 2)
    piece = (4, SPAN, HEAD)
    attended, grad_q, grad_k, grad_v = pl.pallas_call(
        kernel,
        out_shape=[jax.ShapeDtypeStruct((ROWS, NX * WIDE), BF)] * 2 + [
            jax.ShapeDtypeStruct((2, SPAN, NX * HEAD), BF)] * 2,
        in_specs=[smem] * 2 + [any_spec] * 4,
        out_specs=[any_spec] * 4,
        scratch_shapes=[
            vmem(heads, BF), vmem(heads, BF), vmem(gathered, BF), vmem(gathered, BF),
            vmem(padded, BF), vmem(padded, BF), vmem((UNITS, WINDOW, GROUP * SPAN), BF),
            vmem(windows, F32), vmem(windows, F32), vmem(stage, BF), vmem(stage, BF),
            vmem((2, UNITS, HEAD), jnp.int32), pltpu.SMEM((2, UNITS, HEAD), jnp.int32),
            vmem(ring + piece, BF), vmem(ring + piece, BF), vmem((2, 2) + piece, F32), vmem((2, UNITS, SPAN, HEAD), BF),
            dma((1,)), dma((4,)), dma((4, 3)), dma((4, 3)),
            dma((2, 2)), dma((2, UNITS - 2)), dma((2, UNITS - 2)),
            dma((2,)), dma((2, 3)), dma((2, 3)),
            dma(ring), dma(ring), dma(ring), dma(ring),
        ],
        compiler_params=pltpu.CompilerParams(
            collective_id=0, has_side_effects=True, vmem_limit_bytes=56 * 2 ** 20),
        name="attention",
    )(span_order, doc_lengths, queries, keys.reshape(2, SPAN, NX * HEAD), values.reshape(2, SPAN, NX * HEAD), out_grad)
    results = (attended, grad_q, grad_k.reshape(ROWS, NX * HEAD), grad_v.reshape(ROWS, NX * HEAD))
    return pl.pallas_call(
        hand_over,
        out_shape=[jax.ShapeDtypeStruct(result.shape, BF) for result in results],
        in_specs=[any_spec] * 4,
        out_specs=[any_spec] * 4,
        scratch_shapes=[vmem(result.shape, BF) for result in results] + [dma((4, 4)), dma((4, 4))],
        name="hand_over",
    )(*results)


def solution(mesh):
    rows = P(("grp", "seq"), None)
    return jax.shard_map(
        lambda *args: tuple(on_device(*args)),
        mesh=mesh,
        in_specs=(rows, rows, rows, rows, P("grp"), P("grp")),
        out_specs=(rows, rows, rows, rows),
        check_vma=False,
    )
```
